512 devices in a mesh: dp: 16 (over z), ctx: 32 (over x, y, core).
Axes of the slice: x: 4, y: 4, z: 16, core: 2. Of those that a mesh axis runs over, the one named last changes fastest.
Arguments:
- queries: bfloat16 [16, 4096, 2048], P('dp', 'ctx'), may hold values from -6 to 6
- keys: bfloat16 [16, 4096, 2048], P('dp', 'ctx'), may hold values from -6 to 6
- values: bfloat16 [16, 4096, 2048], P('dp', 'ctx'), may hold values from -6 to 6
- out_grad: bfloat16 [16, 4096, 2048], P('dp', 'ctx'), may hold values from -6 to 6
- map_weight: bfloat16 [16, 128, 128], replicated, may hold values from -0.5 to 0.5
Outputs:
- query_grad: bfloat16 [16, 4096, 2048], P('dp', 'ctx')
- key_grad: bfloat16 [16, 4096, 2048], P('dp', 'ctx')
- value_grad: bfloat16 [16, 4096, 2048], P('dp', 'ctx')
- map_grad: float32 [16, 128, 128], replicated
The draws below stay inside these ranges and needn't reach their ends.
All inputs are finite; a program needn't handle non-finite values.
Results may differ from the reference program's by a relative error of at most 0.0096.
Values sent between devices are 32-bit elements; how exact they have to be, the bound alone decides.
A program may use at most 128 MiB of HBM per device.

```python
import jax
import jax.numpy as jnp
from jax import lax

HEADS = 16
HEAD_DIM = 128
TOK_DEV = 128
DOCS = 16
SEQ = 4096
N_CTX = 32


def shard_levels(stream_key, shape, pieces, low, top_value):
    def one(position, shards_of):
        heights = jax.random.uniform(jax.random.fold_in(jax.random.fold_in(stream_key, 6), position), (shards_of,), jnp.float32, low / len(pieces), top_value / len(pieces))
        return jnp.repeat(jnp.exp(heights), shape[position] // shards_of).reshape((-1,) + (1,) * (len(shape) - position - 1))

    factor_of = one(*pieces[0])
    for cut in pieces[1:]:
        factor_of = factor_of * one(*cut)
    return factor_of


def noise(rng, dims, scale, bound, split=(), dtype=jnp.bfloat16):
    entries = jax.random.normal(rng, dims, jnp.float32) * scale
    if len(split) > 0:
        entries = shard_levels(rng, dims, split, -0.22, 0.18) * entries
    return jnp.clip(entries, min=-bound, max=bound).astype(dtype)


def setup_inputs(seed: int = 0) -> dict:
    arg_keys = jax.random.split(jax.random.key(seed), 6)
    queries = noise(arg_keys[0], (DOCS, SEQ, HEADS * HEAD_DIM), 1.0, 6.0, ((0, 16), (1, 32)))
    keys = noise(arg_keys[1], (DOCS, SEQ, HEADS * HEAD_DIM), 1.0, 6.0, ((0, 16), (1, 32)))
    values = noise(arg_keys[2], (DOCS, SEQ, HEADS * HEAD_DIM), 1.0, 6.0, ((0, 16), (1, 32)))
    out_grad = noise(arg_keys[3], (DOCS, SEQ, HEADS * HEAD_DIM), 1.0, 6.0, ((0, 16), (1, 32)))
    map_weight = noise(arg_keys[4], (HEADS, HEAD_DIM, HEAD_DIM), HEAD_DIM ** -0.5, 0.5)
    return dict(queries=queries, keys=keys, values=values, out_grad=out_grad, map_weight=map_weight)


HIGH = lax.Precision.HIGHEST


def mult(form, left, right):
    return jnp.einsum(form, left.astype(jnp.float32), right.astype(jnp.float32), precision=HIGH)


def rounded(x):
    return lax.optimization_barrier(x.astype(jnp.bfloat16))


def doc_grads(query, key_in, value, grad_out, weight):
    query = query.reshape(SEQ, HEADS, HEAD_DIM)
    key_in = key_in.reshape(SEQ, HEADS, HEAD_DIM)
    value = value.reshape(SEQ, HEADS, HEAD_DIM)
    grad_out = grad_out.astype(jnp.float32).reshape(SEQ, HEADS, HEAD_DIM)
    q_pre = mult("the,hef->thf", query, weight)
    k_pre = mult("the,hef->thf", key_in, weight)
    q_feat = jax.nn.elu(q_pre) + 1.0
    k_feat = jax.nn.elu(k_pre) + 1.0
    q_low = rounded(q_feat)
    k_low = rounded(k_feat)
    place = jnp.arange(TOK_DEV)
    causal = (place[:, None] >= place[None, :]).astype(jnp.float32)

    def blocks(x):
        return x.reshape(N_CTX, TOK_DEV, HEADS, HEAD_DIM)

    def forward_step(carry, block):
        state, keysum = carry
        qf, kf, val = block
        scores = mult("thi,shi->hts", qf, kf) * causal
        score_low = rounded(scores)
        state_low = rounded(state)
        numer = mult("hts,she->the", score_low, val) + mult("thi,hij->thj", qf, state_low)
        denom = jnp.sum(scores, axis=2).T + mult("thi,hi->th", qf, keysum)
        new_state = state + mult("shi,shj->hij", kf, val)
        new_sum = keysum + jnp.sum(kf.astype(jnp.float32), axis=0)
        return (new_state, new_sum), (numer / denom[:, :, None], denom, state_low, keysum, score_low)

    zero_state = jnp.zeros((HEADS, HEAD_DIM, HEAD_DIM), jnp.float32)
    zero_sum = jnp.zeros((HEADS, HEAD_DIM), jnp.float32)
    qb, kb, vb, gb = blocks(q_low), blocks(k_low), blocks(value), blocks(grad_out)
    unused, (attended, denom, state_prev, keysum_prev, score_all) = lax.scan(forward_step, (zero_state, zero_sum), (qb, kb, vb))
    scaled = rounded(gb / denom[..., None])
    weight_den = -jnp.sum(gb * attended, axis=3) / denom

    def backward_step(carry, block):
        later_state, later_sum = carry
        qf, kf, val, scl, wden, sprev, zprev, slow = block
        mixed = rounded((mult("the,she->hts", scl, val) + wden.T[:, :, None]) * causal)
        later_low = rounded(later_state)
        qf_grad = mult("hts,shi->thi", mixed, kf) + mult("the,hie->thi", scl, sprev) + wden[:, :, None] * zprev[None]
        kf_grad = mult("hts,thi->shi", mixed, qf) + mult("shj,hij->shi", val, later_low) + later_sum[None]
        v_grad = mult("hts,the->she", slow, scl) + mult("shi,hie->she", kf, later_low)
        new_state = later_state + mult("thi,thj->hij", qf, scl)
        new_sum = later_sum + mult("th,thi->hi", wden, qf)
        return (new_state, new_sum), (qf_grad, kf_grad, v_grad)

    unused, (qf_grad, kf_grad, v_grad) = lax.scan(backward_step, (zero_state, zero_sum), (qb, kb, vb, scaled, weight_den, state_prev, keysum_prev, score_all), reverse=True)
    qf_grad = qf_grad.reshape(SEQ, HEADS, HEAD_DIM)
    kf_grad = kf_grad.reshape(SEQ, HEADS, HEAD_DIM)
    v_grad = v_grad.reshape(SEQ, HEADS * HEAD_DIM)
    q_pre_grad = rounded(qf_grad * jnp.where(q_pre > 0, 1.0, q_feat))
    k_pre_grad = rounded(kf_grad * jnp.where(k_pre > 0, 1.0, k_feat))
    q_grad = mult("thf,hef->the", q_pre_grad, weight).reshape(SEQ, HEADS * HEAD_DIM)
    k_grad = mult("thf,hef->the", k_pre_grad, weight).reshape(SEQ, HEADS * HEAD_DIM)
    map_term = mult("the,thf->hef", query, q_pre_grad) + mult("the,thf->hef", key_in, k_pre_grad)
    return q_grad, k_grad, v_grad, map_term


def reference(queries, keys, values, out_grad, map_weight):
    def one_doc(items):
        return doc_grads(items[0], items[1], items[2], items[3], map_weight)

    q_grad, k_grad, v_grad, map_terms = lax.map(one_doc, (queries, keys, values, out_grad))
    map_grad = jnp.sum(map_terms, axis=0)
    return (q_grad.astype(jnp.bfloat16), k_grad.astype(jnp.bfloat16), v_grad.astype(jnp.bfloat16), map_grad.astype(jnp.float32))
```

```python
import functools
import math

import jax
import jax.numpy as jnp
from jax import lax
from jax.experimental import pallas as pl
from jax.experimental.pallas import tpu as pltpu
from jax.sharding import PartitionSpec as P

GROUPS = 2
PAIR = 2
F32 = jnp.float32
BF16 = jnp.bfloat16


def nn(a, b):
    return lax.dot_general(a, b, (((1,), (0,)), ((), ())), preferred_element_type=F32)


def nt(a, b):
    return lax.dot_general(a, b, (((1,), (1,)), ((), ())), preferred_element_type=F32)


def tn(a, b):
    return lax.dot_general(a, b, (((0,), (0,)), ((), ())), preferred_element_type=F32)


class Sizes:
    def __init__(self, nz, nctx, heads, dim):
        self.nz = nz
        self.chips = nctx // 2
        self.ny = math.isqrt(self.chips)
        self.heads = heads
        self.half = heads // 2
        self.groups = GROUPS
        self.hc = self.half // GROUPS
        self.dim = dim
        self.rows = dim // self.chips


def scratch(s):
    d, hc, g, n = s.dim, s.hc, s.groups, s.chips
    dma = pltpu.SemaphoreType.DMA
    v = pltpu.VMEM
    return dict(
        qv=v((d, s.heads * d), BF16), kv=v((d, s.heads * d), BF16), vv=v((d, s.heads * d), BF16),
        gv=v((d, s.heads * d), BF16), wv=v((s.heads, d, d), BF16),
        qf=v((s.heads, d, d), BF16), kf=v((s.heads, d, d), BF16),
        dq=v((s.heads, d, d), F32), dk=v((s.heads, d, d), F32),
        sc=v((s.heads, d, d), BF16), scaled=v((s.heads, d, d), BF16),
        numer=v((s.heads, d, d), F32), denom=v((s.heads, d, 1), F32), wden=v((s.heads, d, 1), F32),
        kpart=v((s.heads, d, d), F32), vpart=v((s.heads, d, d), F32),
        own=v((3, s.heads, d, d), F32), ksown=v((2, 2, g, 8, d), F32),
        xr=v((3, s.half, d, d), F32), xk=v((2, g, 8, d), F32),
        comb=v((3, g, hc + 1, d, d), F32), recv=v((3, g, n, hc + 1, s.rows, d), F32),
        back=v((2, g, hc, d, d), F32), sib=v((2, g, hc, d, d), F32), ksib=v((2, g, 8, d), F32),
        state=v((2, s.heads, d, d), F32), kstate=v((2, 2, g, 8, d), F32),
        tsum=v((g, hc, s.rows, d), F32), zr=v((g, s.nz, s.rows, d), F32), fin=v((g, hc, s.rows, d), F32),
        qo=v((d, s.heads * d), BF16), ko=v((d, s.heads * d), BF16), vo=v((d, s.heads * d), BF16),
        mo=v((s.heads, d, d), F32),
        in_sem=dma((5,)), out_sem=dma((4,)),
        xs_sem=dma((3, s.half)), xr_sem=dma((3, s.half)), xks_sem=dma((2, g)), xkr_sem=dma((2, g)),
        as_sem=dma((3, g)), ar_sem=dma((3, g)),
        bs_sem=dma((3, g)), br_sem=dma((3, g, n)),
        ys_sem=dma((3, g)), yr_sem=dma((3, g)), yks_sem=dma((2, g)), ykr_sem=dma((2, g)),
        z1s_sem=dma((g,)), z1r_sem=dma((g,)), z2s_sem=dma((g,)), z2r_sem=dma((g,)),
    )


def kernel(s, names, q_hbm, k_hbm, v_hbm, g_hbm, w_hbm, qg_hbm, kg_hbm, vg_hbm, mg_hbm, *refs):
    r = dict(zip(names, refs))
    n, hc, d, half, rows = s.chips, s.hc, s.dim, s.half, s.rows
    z = lax.axis_index("dp")
    ctx = lax.axis_index("ctx")
    core = lax.rem(ctx, 2)
    chip = lax.div(ctx, 2)
    cx, cy = lax.div(chip, s.ny), lax.rem(chip, s.ny)
    coref = core.astype(F32)
    sibling = (z, chip * 2 + 1 - core)

    def peer(step):
        px = lax.rem(cx + lax.div(step, s.ny), s.ny)
        py = lax.rem(cy + lax.rem(step, s.ny), s.ny)
        return px * s.ny + py

    def source(step):
        px = lax.rem(cx + s.ny - lax.div(step, s.ny), s.ny)
        py = lax.rem(cy + s.ny - lax.rem(step, s.ny), s.ny)
        return px * s.ny + py

    def remote(src, dst, send, recv, device):
        return pltpu.make_async_remote_copy(
            src_ref=src, dst_ref=dst, send_sem=send, recv_sem=recv, device_id=device,
            device_id_type=pl.DeviceIdType.MESH)

    def wait_for(ref, sem):
        pltpu.make_async_copy(ref, ref, sem).wait()

    def rows_of(owner):
        return pl.ds(pl.multiple_of(owner * rows, rows), rows)

    def loop(lower, upper, body):
        def step(i, carry):
            body(i)
            return carry

        lax.fori_loop(lower, upper, step, 0)

    barrier = pltpu.get_barrier_semaphore()

    def greet(device):
        pl.semaphore_signal(barrier, inc=1, device_id=device, device_id_type=pl.DeviceIdType.MESH)

    greet(sibling)
    loop(1, n, lambda i: greet((z, peer(i) * 2 + core)))
    loop(1, s.nz, lambda i: greet((lax.rem(z + i, s.nz), ctx)))

    loads = [
        pltpu.make_async_copy(src, dst, r["in_sem"].at[i])
        for i, (src, dst) in enumerate((
            (w_hbm, r["wv"]), (k_hbm.at[0], r["kv"]), (v_hbm.at[0], r["vv"]), (q_hbm.at[0], r["qv"]),
            (g_hbm.at[0], r["gv"])))
    ]
    for load in loads:
        load.start()
    r["ksown"][...] = jnp.zeros_like(r["ksown"])
    for load in loads[:4]:
        load.wait()
    pl.semaphore_wait(barrier, n + s.nz - 1)

    place_t = lax.broadcasted_iota(jnp.int32, (d, d), 0)
    place_s = lax.broadcasted_iota(jnp.int32, (d, d), 1)
    causal = place_t >= place_s

    def columns(h):
        return pl.ds(pl.multiple_of(h * d, d), d)

    def heads_of(g, stage):
        def outer(rel):
            part = rel * core + (1 - rel) * (1 - core)

            def inner(j):
                todo = []
                for e in range(PAIR):
                    i = j * PAIR + e
                    slot = g * hc + i
                    todo.append(stage(rel, i, slot, rel * half + slot, part * half + slot))
                while todo:
                    todo = [t for t in todo if next(t, None) is not None]

            loop(0, hc // PAIR, inner)

        loop(0, 2, outer)

    def send_term(phase, rel, slot, u):
        @pl.when(rel == 0)
        def _():
            remote(r["own"].at[phase, u], r["xr"].at[phase, slot], r["xs_sem"].at[phase, slot],
                   r["xr_sem"].at[phase, slot], sibling).start()

    def features(g):
        def stage(rel, i, slot, u, h):
            w = r["wv"][h]
            val = r["vv"][:, columns(h)]
            k_pre = nn(r["kv"][:, columns(h)], w)
            yield 1
            k_feat = jnp.where(k_pre > 0, k_pre + 1.0, jnp.exp(jnp.minimum(k_pre, 0.0)))
            kf = k_feat.astype(BF16)
            r["kf"][u] = kf
            r["dk"][u] = jnp.minimum(k_feat, 1.0)
            yield 1
            r["own"][0, u] = tn(kf, val)
            r["ksown"][0, rel, g, pl.ds(i, 1), :] = jnp.sum(kf.astype(F32), axis=0, keepdims=True)
            yield 1
            send_term(0, rel, slot, u)
            yield 1
            q_pre = nn(r["qv"][:, columns(h)], w)
            yield 1
            q_feat = jnp.where(q_pre > 0, q_pre + 1.0, jnp.exp(jnp.minimum(q_pre, 0.0)))
            r["qf"][u] = q_feat.astype(BF16)
            r["dq"][u] = jnp.minimum(q_feat, 1.0)

        heads_of(g, stage)
        send_keysum(0, g)

    def send_keysum(phase, g):
        remote(r["ksown"].at[phase, 0, g], r["xk"].at[phase, g], r["xks_sem"].at[phase, g],
               r["xkr_sem"].at[phase, g], sibling).start()

    def combine(phase, g):
        tiles = hc + 1 if phase < 2 else hc

        def one(i):
            wait_for(r["xr"].at[phase, g * hc + i], r["xr_sem"].at[phase, g * hc + i])
            r["comb"][phase, g, i] = r["own"][phase, half + g * hc + i] + r["xr"][phase, g * hc + i]

        loop(0, hc, one)
        if phase < 2:
            wait_for(r["xk"].at[phase, g], r["xkr_sem"].at[phase, g])
            total = r["ksown"][phase, 1, g] + r["xk"][phase, g]
            r["comb"][phase, g, hc] = jnp.concatenate([total] * (d // 8), axis=0)

        def send(step):
            to = peer(step)
            remote(r["comb"].at[phase, g, pl.ds(0, tiles), rows_of(to), :],
                   r["recv"].at[phase, g, chip, pl.ds(0, tiles)],
                   r["as_sem"].at[phase, g], r["ar_sem"].at[phase, g], (z, to * 2 + core)).start()

        loop(1, n, send)
        r["recv"][phase, g, chip, 0:tiles] = r["comb"][phase, g, 0:tiles, rows_of(chip), :]

    def wait_rows(phase, g, sem):
        tiles = hc + 1 if phase < 2 else hc
        wait_for(r["recv"].at[phase, g, pl.ds(0, n - 1), pl.ds(0, tiles)], sem)

    def scan(phase, g):
        wait_rows(phase, g, r["ar_sem"].at[phase, g])
        recv = r["recv"]
        acc = jnp.zeros((hc, rows, d), F32)
        ks = jnp.zeros((8, d), F32)
        for i in range(n) if phase == 0 else reversed(range(n)):
            now = recv[phase, g, i, 0:hc]
            recv[phase, g, i, 0:hc] = acc
            acc = acc + now
            before = (chip > i) if phase == 0 else (chip < i)
            ks = ks + jnp.where(before, recv[phase, g, i, hc, 0:8, :], 0.0)

        def send(step):
            to = peer(step)
            remote(recv.at[phase, g, to, pl.ds(0, hc)],
                   r["back"].at[phase, g, :, rows_of(chip), :],
                   r["bs_sem"].at[phase, g], r["br_sem"].at[phase, g, chip], (z, to * 2 + core)).start()

        loop(1, n, send)
        r["back"][phase, g, :, rows_of(chip), :] = recv[phase, g, chip, 0:hc]
        mine = coref if phase == 0 else 1.0 - coref
        r["kstate"][phase, 1, g] = ks + mine * r["xk"][phase, g]
        r["ksib"][phase, g] = ks + (1.0 - mine) * r["ksown"][phase, 1, g]
        remote(r["ksib"].at[phase, g], r["kstate"].at[phase, 0, g], r["yks_sem"].at[phase, g],
               r["ykr_sem"].at[phase, g], sibling).start()

    def share(phase, g):
        mine = coref if phase == 0 else 1.0 - coref

        def one(step):
            owner = source(step)

            @pl.when(step > 0)
            def _():
                wait_for(r["back"].at[phase, g, :, rows_of(owner), :], r["br_sem"].at[phase, g, owner])

            at = rows_of(owner)
            part = r["back"][phase, g, :, at, :]
            own = r["own"][phase, pl.ds(half + g * hc, hc), at, :]
            other = r["xr"][phase, pl.ds(g * hc, hc), at, :]
            r["state"][phase, pl.ds(half + g * hc, hc), at, :] = part + mine * other
            r["sib"][phase, g, :, at, :] = part + (1.0 - mine) * own
            remote(r["sib"].at[phase, g, :, at, :], r["state"].at[phase, pl.ds(g * hc, hc), at, :],
                   r["ys_sem"].at[phase, g], r["yr_sem"].at[phase, g], sibling).start()

        loop(0, n, one)

    def shared(phase, g):
        wait_for(r["state"].at[phase, pl.ds(g * hc, hc)], r["yr_sem"].at[phase, g])
        wait_for(r["kstate"].at[phase, 0, g], r["ykr_sem"].at[phase, g])

    def local_scores(g):
        def stage(rel, i, slot, u, h):
            scores = nt(r["qf"][u], r["kf"][u])
            yield 1
            scores = jnp.where(causal, scores, 0.0)
            r["denom"][u] = jnp.sum(scores, axis=1, keepdims=True)
            low = scores.astype(BF16)
            r["sc"][u] = low
            yield 1
            r["numer"][u] = nn(low, r["vv"][:, columns(h)])

        heads_of(g, stage)

    def attend(g):
        shared(0, g)

        def stage(rel, i, slot, u, h):
            qf = r["qf"][u]
            grad = r["gv"][:, columns(h)].astype(F32)
            keysum = r["kstate"][0, rel, g, pl.ds(i, 1), :]
            numer = r["numer"][u] + nn(qf, r["state"][0, u].astype(BF16))
            qff = qf.astype(F32)
            denom = r["denom"][u] + jnp.sum(qff * keysum, axis=1, keepdims=True)
            yield 1
            inv = 1.0 / denom
            scaled = (grad * inv).astype(BF16)
            r["scaled"][u] = scaled
            wden = -jnp.sum(grad * (numer * inv), axis=1, keepdims=True) * inv
            r["wden"][u] = wden
            yield 1
            r["own"][1, u] = tn(qf, scaled)
            r["ksown"][1, rel, g, pl.ds(i, 1), :] = jnp.sum(wden * qff, axis=0, keepdims=True)
            yield 1
            send_term(1, rel, slot, u)

        heads_of(g, stage)
        send_keysum(1, g)

    def query_side(g):
        def stage(rel, i, slot, u, h):
            wden = r["wden"][u]
            scaled = r["scaled"][u]
            kf = r["kf"][u]
            keysum = r["kstate"][0, rel, g, pl.ds(i, 1), :]
            mixed = nt(scaled, r["vv"][:, columns(h)])
            yield 1
            mixed = jnp.where(causal, mixed + wden, 0.0).astype(BF16)
            yield 1
            grad = nn(mixed, kf) + nt(scaled, r["state"][0, u].astype(BF16)) + wden * keysum
            yield 1
            pre = (grad * r["dq"][u]).astype(BF16)
            yield 1
            r["qo"][:, columns(h)] = nt(pre, r["wv"][h]).astype(BF16)
            r["own"][2, u] = tn(r["qv"][:, columns(h)], pre)
            yield 1
            r["kpart"][u] = tn(mixed, r["qf"][u])
            r["vpart"][u] = tn(r["sc"][u], scaled)

        heads_of(g, stage)

    def key_side(g):
        shared(1, g)

        def stage(rel, i, slot, u, h):
            later = r["state"][1, u].astype(BF16)
            latersum = r["kstate"][1, rel, g, pl.ds(i, 1), :]
            grad = r["kpart"][u] + nt(r["vv"][:, columns(h)], later) + latersum
            yield 1
            pre = (grad * r["dk"][u]).astype(BF16)
            yield 1
            r["own"][2, u] = r["own"][2, u] + tn(r["kv"][:, columns(h)], pre)
            yield 1
            send_term(2, rel, slot, u)
            yield 1
            r["ko"][:, columns(h)] = nt(pre, r["wv"][h]).astype(BF16)
            r["vo"][:, columns(h)] = (r["vpart"][u] + nn(r["kf"][u], later)).astype(BF16)

        heads_of(g, stage)

    def sum_chips(g):
        wait_rows(2, g, r["ar_sem"].at[2, g])
        acc = r["recv"][2, g, 0, 0:hc]
        for i in range(1, n):
            acc = acc + r["recv"][2, g, i, 0:hc]
        r["tsum"][g] = acc

        def send(step):
            to = lax.rem(z + step, s.nz)
            remote(r["tsum"].at[g, lax.rem(to, hc)], r["zr"].at[g, z], r["z1s_sem"].at[g],
                   r["z1r_sem"].at[g], (to, ctx)).start()

        loop(1, s.nz, send)
        r["zr"][g, z] = r["tsum"][g, lax.rem(z, hc)]

    def sum_docs(g):
        wait_for(r["zr"].at[g, pl.ds(0, s.nz - 1)], r["z1r_sem"].at[g])
        acc = r["zr"][g, 0]
        for i in range(1, s.nz):
            acc = acc + r["zr"][g, i]
        tile = lax.rem(z, hc)
        r["fin"][g, tile] = acc
        for off in range(-(hc // 2), hc - hc // 2):
            if off != 0:
                to = lax.rem(z + s.nz + off, s.nz)
                remote(r["fin"].at[g, tile], r["fin"].at[g, tile], r["z2s_sem"].at[g],
                       r["z2r_sem"].at[g], (to, ctx)).start()

    def to_sibling(g, owner):
        heads = pl.ds(core * half + g * hc, hc)
        block = r["mo"].at[heads, rows_of(owner), :]
        remote(block, block, r["ys_sem"].at[2, g], r["yr_sem"].at[2, g], sibling).start()

    def spread(g):
        heads = pl.ds(core * half + g * hc, hc)
        wait_for(r["fin"].at[g, pl.ds(0, hc - 1)], r["z2r_sem"].at[g])

        def send(step):
            to = peer(step)
            remote(r["fin"].at[g], r["mo"].at[heads, rows_of(chip), :], r["bs_sem"].at[2, g],
                   r["br_sem"].at[2, g, chip], (z, to * 2 + core)).start()

        loop(1, n, send)
        r["mo"][heads, rows_of(chip), :] = r["fin"][g]
        to_sibling(g, chip)

    def collect(g):
        heads = pl.ds(core * half + g * hc, hc)

        def one(step):
            owner = source(step)
            wait_for(r["mo"].at[heads, rows_of(owner), :], r["br_sem"].at[2, g, owner])
            to_sibling(g, owner)

        loop(1, n, one)

    groups = range(s.groups)
    for g in groups:
        features(g)
        if g > 0:
            combine(0, g - 1)
    combine(0, s.groups - 1)
    for g in groups:
        local_scores(g)
        scan(0, g)
    loads[4].wait()
    for g in groups:
        share(0, g)
        attend(g)
        if g > 0:
            combine(1, g - 1)
    combine(1, s.groups - 1)
    for g in groups:
        query_side(g)
        scan(1, g)
    stores = [pltpu.make_async_copy(r["qo"], qg_hbm.at[0], r["out_sem"].at[0])]
    stores[0].start()
    for g in groups:
        share(1, g)
        key_side(g)
        if g > 0:
            combine(2, g - 1)
    combine(2, s.groups - 1)
    stores.append(pltpu.make_async_copy(r["ko"], kg_hbm.at[0], r["out_sem"].at[1]))
    stores.append(pltpu.make_async_copy(r["vo"], vg_hbm.at[0], r["out_sem"].at[2]))
    stores[1].start()
    stores[2].start()
    for g in groups:
        sum_chips(g)
    for g in groups:
        sum_docs(g)
    for g in groups:
        spread(g)
    for g in groups:
        collect(g)
    other = (1 - core) * half
    for g in groups:
        wait_for(r["mo"].at[pl.ds(other + g * hc, hc)], r["yr_sem"].at[2, g])
    stores.append(pltpu.make_async_copy(r["mo"], mg_hbm, r["out_sem"].at[3]))
    stores[3].start()

    for phase in range(3):
        tiles = hc + 1 if phase < 2 else hc
        for slot in range(half):
            wait_for(r["own"].at[phase, slot], r["xs_sem"].at[phase, slot])
        for g in groups:
            wait_for(r["recv"].at[phase, g, pl.ds(0, n - 1), pl.ds(0, tiles)], r["as_sem"].at[phase, g])
            wait_for(r["recv"].at[phase, g, pl.ds(0, n - 1), pl.ds(0, hc)], r["bs_sem"].at[phase, g])
            wait_for(r["mo"].at[pl.ds(0, hc)], r["ys_sem"].at[phase, g])
            if phase < 2:
                wait_for(r["xk"].at[phase, g], r["xks_sem"].at[phase, g])
                wait_for(r["ksib"].at[phase, g], r["yks_sem"].at[phase, g])
    for g in groups:
        wait_for(r["zr"].at[g, pl.ds(0, s.nz - 1)], r["z1s_sem"].at[g])
        wait_for(r["fin"].at[g, pl.ds(0, hc - 1)], r["z2s_sem"].at[g])
    for store in stores:
        store.wait()


def solution(mesh):
    nz, nctx = mesh.shape["dp"], mesh.shape["ctx"]

    def per_device(queries, keys, values, out_grad, map_weight):
        heads, dim = map_weight.shape[0], map_weight.shape[1]
        s = Sizes(nz, nctx, heads, dim)
        spaces = scratch(s)
        act = jax.ShapeDtypeStruct(queries.shape, BF16)
        return pl.pallas_call(
            functools.partial(kernel, s, tuple(spaces)),
            out_shape=(act, act, act, jax.ShapeDtypeStruct(map_weight.shape, F32)),
            in_specs=[pl.BlockSpec(memory_space=pl.ANY)] * 5,
            out_specs=(pl.BlockSpec(memory_space=pl.ANY),) * 4,
            scratch_shapes=list(spaces.values()),
            compiler_params=pltpu.CompilerParams(
                collective_id=0, has_side_effects=True, vmem_limit_bytes=48 * 1024 * 1024),
            cost_estimate=pl.CostEstimate(
                flops=36 * heads * dim**3, bytes_accessed=5 * 1024 * 1024, transcendentals=2 * heads * dim**2),
        )(queries, keys, values, out_grad, map_weight)

    split = P("dp", "ctx", None)
    return jax.shard_map(
        per_device, mesh=mesh, in_specs=(split, split, split, split, P()),
        out_specs=(split, split, split, P()), check_vma=False)
```

```python
import functools
import math

import jax
import jax.numpy as jnp
from jax import lax
from jax.experimental import pallas as pl
from jax.experimental.pallas import tpu as pltpu
from jax.sharding import PartitionSpec as P

GROUPS = 2
F32 = jnp.float32
BF16 = jnp.bfloat16


def nn(a, b):
    return lax.dot_general(a, b, (((1,), (0,)), ((), ())), preferred_element_type=F32)


def nt(a, b):
    return lax.dot_general(a, b, (((1,), (1,)), ((), ())), preferred_element_type=F32)


def tn(a, b):
    return lax.dot_general(a, b, (((0,), (0,)), ((), ())), preferred_element_type=F32)


class Sizes:
    def __init__(self, nz, nctx, heads, dim):
        self.nz = nz
        self.chips = nctx // 2
        self.ny = math.isqrt(self.chips)
        self.heads = heads
        self.half = heads // 2
        self.groups = GROUPS
        self.hc = self.half // GROUPS
        self.dim = dim
        self.rows = dim // self.chips
        near = lambda a, size: min(a, size - a)
        self.plane = sorted(
            ((a, b) for a in range(self.ny) for b in range(self.ny) if a or b),
            key=lambda t: -near(t[0], self.ny) - near(t[1], self.ny))
        self.along = sorted(range(1, nz), key=lambda a: -near(a, nz))


def scratch(s):
    d, hc, g, n, hf = s.dim, s.hc, s.groups, s.chips, s.half
    dma = pltpu.SemaphoreType.DMA
    v = pltpu.VMEM
    wide = hf * d
    return dict(
        xin=v((4, 2, d, wide), BF16), xout=v((4, d, wide), BF16), wv=v((hf, d, d), BF16),
        swap=v((4, d, wide), F32), got=v((4, d, wide), F32),
        qf=v((2, hf, d, d), BF16), kf=v((2, hf, d, d), BF16),
        dq=v((2, hf, d, d), F32), dk=v((2, hf, d, d), F32),
        sc=v((2, hf, d, d), BF16), scaled=v((2, hf, d, d), BF16), kpre=v((2, hf, d, d), BF16),
        numer=v((2, hf, d, d), F32), denom=v((2, hf, d, 1), F32), wden=v((2, hf, d, 1), F32),
        kpart=v((2, hf, d, d), F32), vpart=v((2, hf, d, d), F32),
        own=v((3, 2, hf, d, d), F32), ksown=v((2, 2, g, 8, d), F32),
        comb=v((3, g, hc + 1, d, d), F32), recv=v((3, g, n, hc + 1, s.rows, d), F32),
        back=v((2, g, hc, d, d), F32), kback=v((2, g, 8, d), F32),
        tsum=v((g, hc, s.rows, d), F32), zr=v((g, s.nz, s.rows, d), F32), fin=v((g, hc, s.rows, d), F32),
        outs=v((3, 2, d, wide), F32), outr=v((3, d, wide), F32),
        in_sem=dma((9,)), sws_sem=dma((4,)), swr_sem=dma((4,)), os_sem=dma((3,)), or_sem=dma((3,)),
        as_sem=dma((3, g)), ar_sem=dma((3, g)),
        bs_sem=dma((3, g)), br_sem=dma((2, g)), mr_sem=dma((g, s.ny)),
        ys_sem=dma((g,)), yr_sem=dma((g,)),
        z1s_sem=dma((g,)), z1r_sem=dma((g,)), z2s_sem=dma((g,)), z2r_sem=dma((g,)),
    )


KEY, VALUE, QUERY, GRAD = range(4)


def kernel(s, names, q_hbm, k_hbm, v_hbm, g_hbm, w_hbm, qo, ko, vo, mo, *refs):
    r = dict(zip(names, refs))
    n, hc, d, half, rows, ny = s.chips, s.hc, s.dim, s.half, s.rows, s.ny
    wide = half * d
    z = lax.axis_index("dp")
    ctx = lax.axis_index("ctx")
    core = lax.rem(ctx, 2)
    chip = lax.div(ctx, 2)
    cx, cy = lax.div(chip, ny), lax.rem(chip, ny)
    sibling = (z, chip * 2 + 1 - core)
    groups = range(s.groups)

    def wrap(a, size):
        return jnp.where(a >= size, a - size, a)

    peers = [wrap(cx + a, ny) * ny + wrap(cy + b, ny) for a, b in s.plane]
    depths = [wrap(z + a, s.nz) for a in s.along]

    def remote(src, dst, send, recv, device):
        return pltpu.make_async_remote_copy(
            src_ref=src, dst_ref=dst, send_sem=send, recv_sem=recv, device_id=device,
            device_id_type=pl.DeviceIdType.MESH)

    def wait_for(ref, sem):
        pltpu.make_async_copy(ref, ref, sem).wait()

    def rows_of(owner):
        return pl.ds(pl.multiple_of(owner * rows, rows), rows)

    def half_of(which):
        return pl.ds(pl.multiple_of(which * wide, wide), wide)

    barrier = pltpu.get_barrier_semaphore()

    def greet(device):
        pl.semaphore_signal(barrier, inc=1, device_id=device, device_id_type=pl.DeviceIdType.MESH)

    for to in depths:
        greet((to, ctx))
    for to in peers:
        greet((z, to * 2 + core))
    greet(sibling)

    inputs = (k_hbm, v_hbm, q_hbm, g_hbm)
    away = [pltpu.make_async_copy(x.at[0, :, half_of(1 - core)], r["xout"].at[a], r["in_sem"].at[a])
            for a, x in enumerate(inputs)]
    home = [pltpu.make_async_copy(x.at[0, :, half_of(core)], r["xin"].at[a, core], r["in_sem"].at[4 + a])
            for a, x in enumerate(inputs)]
    load_w = pltpu.make_async_copy(
        w_hbm.at[pl.ds(core * half, half)], r["wv"], r["in_sem"].at[8])
    for load in (away[KEY], away[VALUE], load_w, home[KEY], home[VALUE], away[QUERY], away[GRAD], home[QUERY],
                 home[GRAD]):
        load.start()
    r["ksown"][...] = jnp.zeros_like(r["ksown"])

    def swap_out(a):
        away[a].wait()
        r["swap"][a] = r["xout"][a].astype(F32)

    def swap_send(a):
        for part in range(2):
            at = pl.ds(part * (d // 2), d // 2)
            remote(r["swap"].at[a, at], r["got"].at[a, at], r["sws_sem"].at[a], r["swr_sem"].at[a], sibling).start()

    def swap_in(a):
        wait_for(r["got"].at[a], r["swr_sem"].at[a])
        r["xin"][a, 1 - core] = r["got"][a].astype(BF16)

    place_t = lax.broadcasted_iota(jnp.int32, (d, d), 0)
    place_s = lax.broadcasted_iota(jnp.int32, (d, d), 1)
    causal = place_t >= place_s

    def block(a, b, u):
        return r["xin"][a, b, :, u * d:(u + 1) * d]

    def heads_of(g, stage, blocks=(0, 1)):
        todo = [stage(b, i, g * hc + i) for b in blocks for i in range(hc)]
        while todo:
            todo = [t for t in todo if next(t, None) is not None]

    def key_features(g, b):
        def stage(b, i, u):
            k_pre = nn(block(KEY, b, u), r["wv"][u])
            yield 1
            k_feat = jnp.where(k_pre > 0, k_pre + 1.0, jnp.exp(jnp.minimum(k_pre, 0.0)))
            kf = k_feat.astype(BF16)
            r["kf"][b, u] = kf
            r["dk"][b, u] = jnp.minimum(k_feat, 1.0)
            yield 1
            r["own"][0, b, u] = tn(kf, block(VALUE, b, u))
            r["ksown"][0, b, g, i:i + 1, :] = jnp.sum(kf.astype(F32), axis=0, keepdims=True)

        heads_of(g, stage, (b,))

    def send_rows(phase, g):
        tiles = hc + 1 if phase < 2 else hc
        for i in range(hc):
            u = g * hc + i
            r["comb"][phase, g, i] = r["own"][phase, 0, u] + r["own"][phase, 1, u]
        if phase < 2:
            total = r["ksown"][phase, 0, g] + r["ksown"][phase, 1, g]
            r["comb"][phase, g, hc] = jnp.concatenate([total] * (d // 8), axis=0)
        for to in peers:
            remote(r["comb"].at[phase, g, pl.ds(0, tiles), rows_of(to), :],
                   r["recv"].at[phase, g, chip, pl.ds(0, tiles)],
                   r["as_sem"].at[phase, g], r["ar_sem"].at[phase, g], (z, to * 2 + core)).start()
        r["recv"][phase, g, chip, 0:tiles] = r["comb"][phase, g, 0:tiles, rows_of(chip), :]

    def wait_rows(phase, g, sem):
        tiles = hc + 1 if phase < 2 else hc
        wait_for(r["recv"].at[phase, g, pl.ds(0, n - 1), pl.ds(0, tiles)], sem)

    def scan(phase, g):
        wait_rows(phase, g, r["ar_sem"].at[phase, g])
        recv = r["recv"]
        acc = jnp.zeros((hc, rows, d), F32)
        for i in range(n) if phase == 0 else reversed(range(n)):
            now = recv[phase, g, i, 0:hc]
            recv[phase, g, i, 0:hc] = acc
            acc = acc + now
        for to in peers:
            remote(recv.at[phase, g, to, pl.ds(0, hc)],
                   r["back"].at[phase, g, :, rows_of(chip), :],
                   r["bs_sem"].at[phase, g], r["br_sem"].at[phase, g], (z, to * 2 + core)).start()
        r["back"][phase, g, :, rows_of(chip), :] = recv[phase, g, chip, 0:hc]
        ks = jnp.zeros((8, d), F32)
        for i in range(n):
            before = (chip > i) if phase == 0 else (chip < i)
            ks = ks + jnp.where(before, recv[phase, g, i, hc, 0:8, :], 0.0)
        r["kback"][phase, g] = ks

    def returned(phase, g):
        wait_for(r["back"].at[phase, g, :, pl.ds(0, (n - 1) * rows), :], r["br_sem"].at[phase, g])

    def state_of(phase, b, g, i):
        state = r["back"][phase, g, i]
        if b != phase:
            state = state + r["own"][phase, phase, g * hc + i]
        return state.astype(BF16)

    def sum_of(phase, b, g, i):
        total = r["kback"][phase, g, i:i + 1, :]
        if b != phase:
            total = total + r["ksown"][phase, phase, g, i:i + 1, :]
        return total

    def local_scores(g, blocks=(0, 1)):
        def stage(b, i, u):
            q_pre = nn(block(QUERY, b, u), r["wv"][u])
            yield 1
            q_feat = jnp.where(q_pre > 0, q_pre + 1.0, jnp.exp(jnp.minimum(q_pre, 0.0)))
            qf = q_feat.astype(BF16)
            r["qf"][b, u] = qf
            r["dq"][b, u] = jnp.minimum(q_feat, 1.0)
            yield 1
            scores = nt(qf, r["kf"][b, u])
            yield 1
            scores = jnp.where(causal, scores, 0.0)
            r["denom"][b, u] = jnp.sum(scores, axis=1, keepdims=True)
            low = scores.astype(BF16)
            r["sc"][b, u] = low
            yield 1
            r["numer"][b, u] = nn(low, block(VALUE, b, u))

        heads_of(g, stage, blocks)

    def attend(g):
        def stage(b, i, u):
            qf = r["qf"][b, u]
            grad = block(GRAD, b, u).astype(F32)
            numer = r["numer"][b, u] + nn(qf, state_of(0, b, g, i))
            qff = qf.astype(F32)
            denom = r["denom"][b, u] + jnp.sum(qff * sum_of(0, b, g, i), axis=1, keepdims=True)
            yield 1
            inv = 1.0 / denom
            scaled = (grad * inv).astype(BF16)
            r["scaled"][b, u] = scaled
            wden = -jnp.sum(grad * (numer * inv), axis=1, keepdims=True) * inv
            r["wden"][b, u] = wden
            yield 1
            r["own"][1, b, u] = tn(qf, scaled)
            r["ksown"][1, b, g, i:i + 1, :] = jnp.sum(wden * qff, axis=0, keepdims=True)

        heads_of(g, stage)

    def query_side(g, blocks=(0, 1)):
        def stage(b, i, u):
            wden = r["wden"][b, u]
            scaled = r["scaled"][b, u]
            mixed = nt(scaled, block(VALUE, b, u))
            yield 1
            mixed = jnp.where(causal, mixed + wden, 0.0).astype(BF16)
            yield 1
            grad = nn(mixed, r["kf"][b, u]) + nt(scaled, state_of(0, b, g, i)) + wden * sum_of(0, b, g, i)
            yield 1
            pre = (grad * r["dq"][b, u]).astype(BF16)
            yield 1
            r["outs"][0, b, :, u * d:(u + 1) * d] = nt(pre, r["wv"][u])
            r["own"][2, b, u] = tn(block(QUERY, b, u), pre)
            yield 1
            r["kpart"][b, u] = tn(mixed, r["qf"][b, u])
            r["vpart"][b, u] = tn(r["sc"][b, u], scaled)

        heads_of(g, stage, blocks)

    def key_side(g):
        def stage(b, i, u):
            grad = r["kpart"][b, u] + nt(block(VALUE, b, u), state_of(1, b, g, i)) + sum_of(1, b, g, i)
            yield 1
            pre = (grad * r["dk"][b, u]).astype(BF16)
            r["kpre"][b, u] = pre
            yield 1
            r["own"][2, b, u] = r["own"][2, b, u] + tn(block(KEY, b, u), pre)

        heads_of(g, stage)

    def key_outputs(g):
        def stage(b, i, u):
            r["outs"][1, b, :, u * d:(u + 1) * d] = nt(r["kpre"][b, u], r["wv"][u])
            r["outs"][2, b, :, u * d:(u + 1) * d] = r["vpart"][b, u] + nn(r["kf"][b, u], state_of(1, b, g, i))
            yield 1

        heads_of(g, stage)

    def give_out(a):
        remote(r["outs"].at[a, 1 - core], r["outr"].at[a], r["os_sem"].at[a], r["or_sem"].at[a], sibling).start()
        (qo, ko, vo)[a][0, :, half_of(core)] = r["outs"][a, core].astype(BF16)

    def take_out(a):
        wait_for(r["outr"].at[a], r["or_sem"].at[a])
        (qo, ko, vo)[a][0, :, half_of(1 - core)] = r["outr"][a].astype(BF16)

    def sum_chips(g):
        wait_rows(2, g, r["ar_sem"].at[2, g])
        acc = r["recv"][2, g, 0, 0:hc]
        for i in range(1, n):
            acc = acc + r["recv"][2, g, i, 0:hc]
        r["tsum"][g] = acc
        for to in depths:
            remote(r["tsum"].at[g, lax.rem(to, hc)], r["zr"].at[g, z], r["z1s_sem"].at[g],
                   r["z1r_sem"].at[g], (to, ctx)).start()
        r["zr"][g, z] = r["tsum"][g, lax.rem(z, hc)]

    def sum_docs(g):
        wait_for(r["zr"].at[g, pl.ds(0, s.nz - 1)], r["z1r_sem"].at[g])
        acc = r["zr"][g, 0]
        for i in range(1, s.nz):
            acc = acc + r["zr"][g, i]
        tile = lax.rem(z, hc)
        r["fin"][g, tile] = acc
        for off in range(-(hc // 2), hc - hc // 2):
            if off != 0:
                to = wrap(z + off % s.nz, s.nz)
                remote(r["fin"].at[g, tile], r["fin"].at[g, tile], r["z2s_sem"].at[g],
                       r["z2r_sem"].at[g], (to, ctx)).start()

    def spread(g):
        heads = pl.ds(core * half + g * hc, hc)
        if hc > 1:
            wait_for(r["fin"].at[g, pl.ds(0, hc - 1)], r["z2r_sem"].at[g])
        for to in peers:
            remote(r["fin"].at[g], mo.at[heads, rows_of(chip), :], r["bs_sem"].at[2, g],
                   r["mr_sem"].at[g, cx], (z, to * 2 + core)).start()
        mo[heads, rows_of(chip), :] = r["fin"][g]

    def strips():
        order = [0] + sorted(range(1, ny), key=lambda a: min(a, ny - a))
        for a in order:
            px = wrap(cx + a, ny)
            start = pl.multiple_of(px * (ny * rows), ny * rows)
            yield px, start, (ny if a else ny - 1)

    def collect(g):
        heads = pl.ds(core * half + g * hc, hc)
        for px, start, count in strips():
            wait_for(mo.at[heads, pl.ds(start, count * rows), :], r["mr_sem"].at[g, px])
            part = mo.at[heads, pl.ds(start, ny * rows), :]
            remote(part, part, r["ys_sem"].at[g], r["yr_sem"].at[g], sibling).start()

    first, last = groups[:-1], s.groups - 1
    swap_out(KEY)
    pl.semaphore_wait(barrier, n + s.nz - 1)
    swap_send(KEY)
    swap_out(VALUE)
    swap_send(VALUE)
    load_w.wait()
    home[KEY].wait()
    home[VALUE].wait()
    swap_in(KEY)
    swap_in(VALUE)
    for g in groups:
        key_features(g, 0)
        key_features(g, 1)
        send_rows(0, g)
    for a in (QUERY, GRAD):
        swap_out(a)
        swap_send(a)
        home[a].wait()
    swap_in(QUERY)
    for g in first:
        local_scores(g)
        scan(0, g)
    local_scores(last, (0,))
    scan(0, last)
    local_scores(last, (1,))
    swap_in(GRAD)
    for g in groups:
        returned(0, g)
        attend(g)
        send_rows(1, g)
    query_side(0)
    for g in first:
        query_side(g + 1, (0,))
        scan(1, g)
        query_side(g + 1, (1,))
    scan(1, last)
    give_out(0)
    for g in groups:
        returned(1, g)
        key_side(g)
        send_rows(2, g)
    for g in groups:
        key_outputs(g)
    give_out(1)
    give_out(2)
    for g in groups:
        sum_chips(g)
    for a in range(3):
        take_out(a)
    for g in groups:
        sum_docs(g)
    for g in groups:
        spread(g)
    for g in groups:
        collect(g)
    other = (1 - core) * half
    for g in groups:
        wait_for(mo.at[pl.ds(other + g * hc, hc)], r["yr_sem"].at[g])

    for a in range(4):
        wait_for(r["got"].at[a], r["sws_sem"].at[a])
    for a in range(3):
        wait_for(r["outr"].at[a], r["os_sem"].at[a])
    for g in groups:
        for phase in range(3):
            wait_rows(phase, g, r["as_sem"].at[phase, g])
            wait_for(r["recv"].at[phase, g, pl.ds(0, n - 1), pl.ds(0, hc)], r["bs_sem"].at[phase, g])
        wait_for(mo.at[pl.ds(0, hc)], r["ys_sem"].at[g])
        wait_for(r["zr"].at[g, pl.ds(0, s.nz - 1)], r["z1s_sem"].at[g])
        if hc > 1:
            wait_for(r["fin"].at[g, pl.ds(0, hc - 1)], r["z2s_sem"].at[g])


def write_out(*refs):
    count = len(refs) // 2
    sems = refs[-1]
    copies = []
    for i, (src, dst) in enumerate(zip(refs[:count], refs[count:-1])):
        copies.append(pltpu.make_async_copy(src, dst, sems.at[i]))
    for copy in copies:
        copy.start()
    for copy in copies:
        copy.wait()


def solution(mesh):
    nz, nctx = mesh.shape["dp"], mesh.shape["ctx"]

    def per_device(queries, keys, values, out_grad, map_weight):
        heads, dim = map_weight.shape[0], map_weight.shape[1]
        s = Sizes(nz, nctx, heads, dim)
        spaces = scratch(s)
        act = jax.ShapeDtypeStruct(queries.shape, BF16)
        shapes = (act, act, act, jax.ShapeDtypeStruct(map_weight.shape, F32))
        grads = pl.pallas_call(
            functools.partial(kernel, s, tuple(spaces)),
            out_shape=shapes,
            in_specs=[pl.BlockSpec(memory_space=pltpu.HBM)] * 5,
            out_specs=(pl.BlockSpec(memory_space=pltpu.VMEM),) * 4,
            scratch_shapes=list(spaces.values()),
            compiler_params=pltpu.CompilerParams(
                collective_id=0, has_side_effects=True, vmem_limit_bytes=52 * 1024 * 1024),
            cost_estimate=pl.CostEstimate(
                flops=36 * heads * dim**3, bytes_accessed=5 * 1024 * 1024, transcendentals=2 * heads * dim**2),
        )(queries, keys, values, out_grad, map_weight)
        return pl.pallas_call(
            write_out,
            out_shape=shapes,
            in_specs=[pl.BlockSpec(memory_space=pltpu.VMEM)] * 4,
            out_specs=(pl.BlockSpec(memory_space=pltpu.HBM),) * 4,
            scratch_shapes=[pltpu.SemaphoreType.DMA((4,))],
            compiler_params=pltpu.CompilerParams(vmem_limit_bytes=4 * 1024 * 1024),
        )(*grads)

    split = P("dp", "ctx", None)
    return jax.shard_map(
        per_device, mesh=mesh, in_specs=(split, split, split, split, P()),
        out_specs=(split, split, split, P()), check_vma=False)
```

```python
import functools
import math

import jax
import jax.numpy as jnp
from jax import lax
from jax.experimental import pallas as pl
from jax.experimental.pallas import tpu as pltpu
from jax.sharding import PartitionSpec as P

GROUPS = 2
F32 = jnp.float32
BF16 = jnp.bfloat16


def nn(a, b):
    return lax.dot_general(a, b, (((1,), (0,)), ((), ())), preferred_element_type=F32)


def nt(a, b):
    return lax.dot_general(a, b, (((1,), (1,)), ((), ())), preferred_element_type=F32)


def tn(a, b):
    return lax.dot_general(a, b, (((0,), (0,)), ((), ())), preferred_element_type=F32)


class Sizes:
    def __init__(self, nz, nctx, heads, dim):
        self.nz = nz
        self.chips = nctx // 2
        self.ny = math.isqrt(self.chips)
        self.heads = heads
        self.half = heads // 2
        self.groups = GROUPS
        self.hc = self.half // GROUPS
        self.dim = dim
        self.rows = dim // self.chips
        near = lambda a, size: min(a, size - a)
        self.plane = sorted(
            ((a, b) for a in range(self.ny) for b in range(self.ny) if a or b),
            key=lambda t: -near(t[0], self.ny) - near(t[1], self.ny))
        self.along = sorted(range(1, nz), key=lambda a: -near(a, nz))


def scratch(s):
    d, hc, g, n, hf = s.dim, s.hc, s.groups, s.chips, s.half
    dma = pltpu.SemaphoreType.DMA
    v = pltpu.VMEM
    wide = hf * d
    return dict(
        xin=v((4, 2, d, wide), BF16), xout=v((4, d, wide), BF16), wv=v((hf, d, d), BF16),
        swap=v((4, d, wide), F32), got=v((4, d, wide), F32),
        qf=v((2, hf, d, d), BF16), kf=v((2, hf, d, d), BF16),
        dq=v((2, hf, d, d), F32), dk=v((2, hf, d, d), F32),
        sc=v((2, hf, d, d), BF16), scaled=v((2, hf, d, d), BF16), kpre=v((2, hf, d, d), BF16),
        numer=v((2, hf, d, d), F32), denom=v((2, hf, d, 1), F32), wden=v((2, hf, d, 1), F32),
        kpart=v((2, hf, d, d), F32), vpart=v((2, hf, d, d), F32),
        own=v((3, 2, hf, d, d), F32), ksown=v((2, 2, 8, d), F32),
        comb=v((3, g, hc + 1, d, d), F32), recv=v((3, g, n, hc + 1, s.rows, d), F32),
        back=v((2, g, hc, d, d), F32), kback=v((2, 8, d), F32), mo=v((s.heads, d, d), F32),
        tsum=v((g, hc, s.rows, d), F32), zr=v((g, s.nz, s.rows, d), F32), fin=v((g, hc, s.rows, d), F32),
        outs=v((3, 2, d, wide), F32), outr=v((3, d, wide), F32),
        in_sem=dma((9,)), out_sem=dma((2, g)), sws_sem=dma((4, g)), swr_sem=dma((4, g)), met_sem=pltpu.SemaphoreType.REGULAR((2,)), os_sem=dma((3,)), or_sem=dma((3,)),
        as_sem=dma((3, g)), ar_sem=dma((3, g)),
        bs_sem=dma((3, g)), br_sem=dma((2, g)), mr_sem=dma((g, s.ny)),
        ys_sem=dma((g,)), yr_sem=dma((g,)),
        z1s_sem=dma((g,)), z1r_sem=dma((g,)), z2s_sem=dma((g,)), z2r_sem=dma((g,)),
    )


KEY, VALUE, QUERY, GRAD = range(4)


def kernel(s, names, q_hbm, k_hbm, v_hbm, g_hbm, w_hbm, qo, ko, vo, mg_hbm, *refs):
    r = dict(zip(names, refs))
    mo = r["mo"]
    n, hc, d, half, rows, ny = s.chips, s.hc, s.dim, s.half, s.rows, s.ny
    wide = half * d
    z = lax.axis_index("dp")
    ctx = lax.axis_index("ctx")
    core = lax.rem(ctx, 2)
    chip = lax.div(ctx, 2)
    cx, cy = lax.div(chip, ny), lax.rem(chip, ny)
    sibling = (z, chip * 2 + 1 - core)
    groups = range(s.groups)

    def wrap(a, size):
        return jnp.where(a >= size, a - size, a)

    peers = [wrap(cx + a, ny) * ny + wrap(cy + b, ny) for a, b in s.plane]
    depths = [wrap(z + a, s.nz) for a in s.along]

    def remote(src, dst, send, recv, device):
        return pltpu.make_async_remote_copy(
            src_ref=src, dst_ref=dst, send_sem=send, recv_sem=recv, device_id=device,
            device_id_type=pl.DeviceIdType.MESH)

    def wait_for(ref, sem):
        pltpu.make_async_copy(ref, ref, sem).wait()

    def rows_of(owner):
        return pl.ds(pl.multiple_of(owner * rows, rows), rows)

    def half_of(which):
        return pl.ds(pl.multiple_of(which * wide, wide), wide)

    barrier = pltpu.get_barrier_semaphore()

    def greet(device):
        pl.semaphore_signal(barrier, inc=1, device_id=device, device_id_type=pl.DeviceIdType.MESH)

    below, above = wrap(z + s.nz - 1, s.nz), wrap(z + 1, s.nz)
    near = (below, above) if s.nz > 2 else (above,)
    for to in near:
        greet((to, ctx))
    for to in peers:
        greet((z, to * 2 + core))
    greet(sibling)

    def meet(turn):
        turns = s.nz // 2 - 1
        if 1 < turn <= turns + 1:
            for i in range(2):
                pl.semaphore_wait(r["met_sem"].at[i], 1)
        if turn <= turns:
            for i, to in enumerate((above, below)):
                pl.semaphore_signal(
                    r["met_sem"].at[i], inc=1, device_id=(to, ctx), device_id_type=pl.DeviceIdType.MESH)

    inputs = (k_hbm, v_hbm, q_hbm, g_hbm)
    away = [pltpu.make_async_copy(x.at[0, :, half_of(1 - core)], r["xout"].at[a], r["in_sem"].at[a])
            for a, x in enumerate(inputs)]
    home = [pltpu.make_async_copy(x.at[0, :, half_of(core)], r["xin"].at[a, core], r["in_sem"].at[4 + a])
            for a, x in enumerate(inputs)]
    load_w = pltpu.make_async_copy(
        w_hbm.at[pl.ds(core * half, half)], r["wv"], r["in_sem"].at[8])
    for load in (away[KEY], away[VALUE], load_w, home[KEY], home[VALUE], away[QUERY], away[GRAD], home[QUERY],
                 home[GRAD]):
        load.start()
    r["ksown"][...] = jnp.zeros_like(r["ksown"])

    def swap_out(a):
        away[a].wait()
        r["swap"][a] = r["xout"][a].astype(F32)

    def swap_send(a, g):
        for part in range(2):
            at = (a, pl.ds(part * (d // 2), d // 2), pl.ds(g * hc * d, hc * d))
            remote(r["swap"].at[at], r["got"].at[at], r["sws_sem"].at[a, g], r["swr_sem"].at[a, g], sibling).start()

    def swap_in(a, g):
        at = slice(g * hc * d, (g + 1) * hc * d)
        wait_for(r["got"].at[a, :, at], r["swr_sem"].at[a, g])
        r["xin"][a, 1 - core, :, at] = r["got"][a, :, at].astype(BF16)

    place_t = lax.broadcasted_iota(jnp.int32, (d, d), 0)
    place_s = lax.broadcasted_iota(jnp.int32, (d, d), 1)
    causal = place_t >= place_s

    def block(a, b, u):
        return r["xin"][a, b, :, u * d:(u + 1) * d]

    def heads_of(g, stage, blocks=(0, 1)):
        todo = [stage(b, i, g * hc + i) for b in blocks for i in range(hc)]
        while todo:
            todo = [t for t in todo if next(t, None) is not None]

    def key_features(g, b):
        def stage(b, i, u):
            k_pre = nn(block(KEY, b, u), r["wv"][u])
            yield 1
            k_feat = jnp.where(k_pre > 0, k_pre + 1.0, jnp.exp(jnp.minimum(k_pre, 0.0)))
            kf = k_feat.astype(BF16)
            r["kf"][b, u] = kf
            r["dk"][b, u] = jnp.minimum(k_feat, 1.0)
            yield 1
            r["own"][0, b, u] = tn(kf, block(VALUE, b, u))
            r["ksown"][0, b, u:u + 1, :] = jnp.sum(kf.astype(F32), axis=0, keepdims=True)

        heads_of(g, stage, (b,))

    def tiles_of(phase, g):
        return hc + 1 if phase < 2 and g == s.groups - 1 else hc

    def send_rows(phase, g):
        tiles = tiles_of(phase, g)
        for i in range(hc):
            u = g * hc + i
            r["comb"][phase, g, i] = r["own"][phase, 0, u] + r["own"][phase, 1, u]
        if tiles > hc:
            total = r["ksown"][phase, 0] + r["ksown"][phase, 1]
            r["comb"][phase, g, hc] = jnp.concatenate([total] * (d // 8), axis=0)
        for to in peers:
            remote(r["comb"].at[phase, g, pl.ds(0, tiles), rows_of(to), :],
                   r["recv"].at[phase, g, chip, pl.ds(0, tiles)],
                   r["as_sem"].at[phase, g], r["ar_sem"].at[phase, g], (z, to * 2 + core)).start()
        r["recv"][phase, g, chip, 0:tiles] = r["comb"][phase, g, 0:tiles, rows_of(chip), :]

    def wait_rows(phase, g, sem):
        wait_for(r["recv"].at[phase, g, pl.ds(0, n - 1), pl.ds(0, tiles_of(phase, g))], sem)

    def scan(phase, g):
        wait_rows(phase, g, r["ar_sem"].at[phase, g])
        recv = r["recv"]
        acc = jnp.zeros((hc, rows, d), F32)
        for i in range(n) if phase == 0 else reversed(range(n)):
            now = recv[phase, g, i, 0:hc]
            recv[phase, g, i, 0:hc] = acc
            acc = acc + now
        for to in peers:
            remote(recv.at[phase, g, to, pl.ds(0, hc)],
                   r["back"].at[phase, g, :, rows_of(chip), :],
                   r["bs_sem"].at[phase, g], r["br_sem"].at[phase, g], (z, to * 2 + core)).start()
        r["back"][phase, g, :, rows_of(chip), :] = recv[phase, g, chip, 0:hc]
        if tiles_of(phase, g) > hc:
            ks = jnp.zeros((8, d), F32)
            for i in range(n):
                before = (chip > i) if phase == 0 else (chip < i)
                ks = ks + jnp.where(before, recv[phase, g, i, hc, 0:8, :], 0.0)
            r["kback"][phase] = ks

    def returned(phase, g):
        wait_for(r["back"].at[phase, g, :, pl.ds(0, (n - 1) * rows), :], r["br_sem"].at[phase, g])

    def state_of(phase, b, g, i):
        state = r["back"][phase, g, i]
        if b != phase:
            state = state + r["own"][phase, phase, g * hc + i]
        return state.astype(BF16)

    def sum_of(phase, b, g, i):
        u = g * hc + i
        total = r["kback"][phase, u:u + 1, :]
        if b != phase:
            total = total + r["ksown"][phase, phase, u:u + 1, :]
        return total

    def local_scores(g, blocks=(0, 1)):
        def stage(b, i, u):
            q_pre = nn(block(QUERY, b, u), r["wv"][u])
            yield 1
            q_feat = jnp.where(q_pre > 0, q_pre + 1.0, jnp.exp(jnp.minimum(q_pre, 0.0)))
            qf = q_feat.astype(BF16)
            r["qf"][b, u] = qf
            r["dq"][b, u] = jnp.minimum(q_feat, 1.0)
            yield 1
            scores = nt(qf, r["kf"][b, u])
            yield 1
            scores = jnp.where(causal, scores, 0.0)
            r["denom"][b, u] = jnp.sum(scores, axis=1, keepdims=True)
            low = scores.astype(BF16)
            r["sc"][b, u] = low
            yield 1
            r["numer"][b, u] = nn(low, block(VALUE, b, u))

        heads_of(g, stage, blocks)

    def attend(g):
        def stage(b, i, u):
            qf = r["qf"][b, u]
            grad = block(GRAD, b, u).astype(F32)
            numer = r["numer"][b, u] + nn(qf, state_of(0, b, g, i))
            qff = qf.astype(F32)
            denom = r["denom"][b, u] + jnp.sum(qff * sum_of(0, b, g, i), axis=1, keepdims=True)
            yield 1
            inv = 1.0 / denom
            scaled = (grad * inv).astype(BF16)
            r["scaled"][b, u] = scaled
            wden = -jnp.sum(grad * (numer * inv), axis=1, keepdims=True) * inv
            r["wden"][b, u] = wden
            yield 1
            r["own"][1, b, u] = tn(qf, scaled)
            r["ksown"][1, b, u:u + 1, :] = jnp.sum(wden * qff, axis=0, keepdims=True)

        heads_of(g, stage)

    def query_side(g, blocks=(0, 1)):
        def stage(b, i, u):
            wden = r["wden"][b, u]
            scaled = r["scaled"][b, u]
            mixed = nt(scaled, block(VALUE, b, u))
            yield 1
            mixed = jnp.where(causal, mixed + wden, 0.0).astype(BF16)
            yield 1
            grad = nn(mixed, r["kf"][b, u]) + nt(scaled, state_of(0, b, g, i)) + wden * sum_of(0, b, g, i)
            yield 1
            pre = (grad * r["dq"][b, u]).astype(BF16)
            yield 1
            r["outs"][0, b, :, u * d:(u + 1) * d] = nt(pre, r["wv"][u])
            r["own"][2, b, u] = tn(block(QUERY, b, u), pre)
            yield 1
            r["kpart"][b, u] = tn(mixed, r["qf"][b, u])
            r["vpart"][b, u] = tn(r["sc"][b, u], scaled)

        heads_of(g, stage, blocks)

    def key_side(g):
        def stage(b, i, u):
            grad = r["kpart"][b, u] + nt(block(VALUE, b, u), state_of(1, b, g, i)) + sum_of(1, b, g, i)
            yield 1
            pre = (grad * r["dk"][b, u]).astype(BF16)
            r["kpre"][b, u] = pre
            yield 1
            r["own"][2, b, u] = r["own"][2, b, u] + tn(block(KEY, b, u), pre)

        heads_of(g, stage)

    def key_outputs(g):
        def stage(b, i, u):
            r["outs"][1, b, :, u * d:(u + 1) * d] = nt(r["kpre"][b, u], r["wv"][u])
            r["outs"][2, b, :, u * d:(u + 1) * d] = r["vpart"][b, u] + nn(r["kf"][b, u], state_of(1, b, g, i))
            yield 1

        heads_of(g, stage)

    def give_out(a):
        remote(r["outs"].at[a, 1 - core], r["outr"].at[a], r["os_sem"].at[a], r["or_sem"].at[a], sibling).start()
        (qo, ko, vo)[a][0, :, half_of(core)] = r["outs"][a, core].astype(BF16)

    def take_out(a):
        wait_for(r["outr"].at[a], r["or_sem"].at[a])
        (qo, ko, vo)[a][0, :, half_of(1 - core)] = r["outr"][a].astype(BF16)

    def sum_chips(g):
        wait_rows(2, g, r["ar_sem"].at[2, g])
        acc = r["recv"][2, g, 0, 0:hc]
        for i in range(1, n):
            acc = acc + r["recv"][2, g, i, 0:hc]
        r["tsum"][g] = acc
        for to in depths:
            remote(r["tsum"].at[g, lax.rem(to, hc)], r["zr"].at[g, z], r["z1s_sem"].at[g],
                   r["z1r_sem"].at[g], (to, ctx)).start()
        r["zr"][g, z] = r["tsum"][g, lax.rem(z, hc)]

    def sum_docs(g):
        wait_for(r["zr"].at[g, pl.ds(0, s.nz - 1)], r["z1r_sem"].at[g])
        acc = r["zr"][g, 0]
        for i in range(1, s.nz):
            acc = acc + r["zr"][g, i]
        tile = lax.rem(z, hc)
        r["fin"][g, tile] = acc
        for off in range(-(hc // 2), hc - hc // 2):
            if off != 0:
                to = wrap(z + off % s.nz, s.nz)
                remote(r["fin"].at[g, tile], r["fin"].at[g, tile], r["z2s_sem"].at[g],
                       r["z2r_sem"].at[g], (to, ctx)).start()

    def spread(g):
        heads = pl.ds(core * half + g * hc, hc)
        if hc > 1:
            wait_for(r["fin"].at[g, pl.ds(0, hc - 1)], r["z2r_sem"].at[g])
        for to in peers:
            remote(r["fin"].at[g], mo.at[heads, rows_of(chip), :], r["bs_sem"].at[2, g],
                   r["mr_sem"].at[g, cx], (z, to * 2 + core)).start()
        mo[heads, rows_of(chip), :] = r["fin"][g]

    def strips():
        order = [0] + sorted(range(1, ny), key=lambda a: min(a, ny - a))
        for a in order:
            px = wrap(cx + a, ny)
            start = pl.multiple_of(px * (ny * rows), ny * rows)
            yield px, start, (ny if a else ny - 1)

    def collect(g):
        heads = pl.ds(core * half + g * hc, hc)
        for px, start, count in strips():
            wait_for(mo.at[heads, pl.ds(start, count * rows), :], r["mr_sem"].at[g, px])
            part = mo.at[heads, pl.ds(start, ny * rows), :]
            remote(part, part, r["ys_sem"].at[g], r["yr_sem"].at[g], sibling).start()

    def store(which, g):
        heads = pl.ds(which * half + g * hc, hc)
        return pltpu.make_async_copy(mo.at[heads], mg_hbm.at[heads], r["out_sem"].at[0 if which is core else 1, g])

    first, last = groups[:-1], s.groups - 1
    swap_out(KEY)
    swap_out(VALUE)
    load_w.wait()
    home[KEY].wait()
    home[VALUE].wait()
    for g in groups:
        key_features(g, core)
    pl.semaphore_wait(barrier, n + len(near))
    for g in groups:
        swap_send(KEY, g)
        swap_send(VALUE, g)
    turn = 0
    for g in groups:
        swap_in(KEY, g)
        swap_in(VALUE, g)
        key_features(g, 1 - core)
        send_rows(0, g)
        turn += 1
        meet(turn)
    for a in (QUERY, GRAD):
        swap_out(a)
        for g in groups:
            swap_send(a, g)
        home[a].wait()
    for g in groups:
        swap_in(QUERY, g)
    for g in first:
        local_scores(g)
        scan(0, g)
        turn += 1
        meet(turn)
    local_scores(last, (0,))
    scan(0, last)
    turn += 1
    meet(turn)
    local_scores(last, (1,))
    for g in groups:
        swap_in(GRAD, g)
    for g in groups:
        returned(0, g)
        attend(g)
        send_rows(1, g)
        turn += 1
        meet(turn)
    query_side(0)
    for g in first:
        query_side(g + 1, (0,))
        scan(1, g)
        turn += 1
        meet(turn)
        query_side(g + 1, (1,))
    scan(1, last)
    give_out(0)
    while turn < s.nz // 2:
        turn += 1
        meet(turn)
    for g in groups:
        returned(1, g)
        key_side(g)
        send_rows(2, g)
    for g in groups:
        key_outputs(g)
    give_out(1)
    give_out(2)
    for g in groups:
        sum_chips(g)
    for a in range(3):
        take_out(a)
    for a in range(4):
        for g in groups:
            wait_for(r["got"].at[a, :, pl.ds(g * hc * d, hc * d)], r["sws_sem"].at[a, g])
    for a in range(3):
        wait_for(r["outr"].at[a], r["os_sem"].at[a])
    for g in groups:
        for phase in range(3):
            wait_rows(phase, g, r["as_sem"].at[phase, g])
        for phase in range(2):
            wait_for(r["recv"].at[phase, g, pl.ds(0, n - 1), pl.ds(0, hc)], r["bs_sem"].at[phase, g])
    for g in groups:
        sum_docs(g)
    for g in groups:
        spread(g)
    for g in groups:
        collect(g)
        store(core, g).start()
    other = 1 - core
    for g in groups:
        wait_for(mo.at[pl.ds(other * half + g * hc, hc)], r["yr_sem"].at[g])
        store(other, g).start()
    for g in groups:
        wait_for(r["recv"].at[2, g, pl.ds(0, n - 1), pl.ds(0, hc)], r["bs_sem"].at[2, g])
        wait_for(mo.at[pl.ds(0, hc)], r["ys_sem"].at[g])
        wait_for(r["zr"].at[g, pl.ds(0, s.nz - 1)], r["z1s_sem"].at[g])
        if hc > 1:
            wait_for(r["fin"].at[g, pl.ds(0, hc - 1)], r["z2s_sem"].at[g])
    for g in groups:
        store(core, g).wait()
        store(other, g).wait()


def write_out(q, k, v, m, qg, kg, vg, mg, sems, held):
    size = m.shape[0] // 4
    parts = [pl.ds(part * size, size) for part in range(4)]
    reads = [pltpu.make_async_copy(m.at[at], held.at[at], sems.at[i]) for i, at in enumerate(parts)]
    writes = [pltpu.make_async_copy(held.at[at], mg.at[at], sems.at[4 + i]) for i, at in enumerate(parts)]
    rows = q.shape[1] // 2
    for src, dst in ((q, qg), (k, kg), (v, vg)):
        for part in range(2):
            at = pl.ds(part * rows, rows)
            writes.append(pltpu.make_async_copy(src.at[0, at], dst.at[0, at], sems.at[4 + len(writes)]))
    for copy in reads + writes[4:]:
        copy.start()
    for read, write in zip(reads, writes):
        read.wait()
        write.start()
    for copy in writes:
        copy.wait()


def solution(mesh):
    nz, nctx = mesh.shape["dp"], mesh.shape["ctx"]

    def per_device(queries, keys, values, out_grad, map_weight):
        heads, dim = map_weight.shape[0], map_weight.shape[1]
        s = Sizes(nz, nctx, heads, dim)
        spaces = scratch(s)
        act = jax.ShapeDtypeStruct(queries.shape, BF16)
        shapes = (act, act, act, jax.ShapeDtypeStruct(map_weight.shape, F32))
        grads = pl.pallas_call(
            functools.partial(kernel, s, tuple(spaces)),
            out_shape=shapes,
            in_specs=[pl.BlockSpec(memory_space=pltpu.HBM)] * 5,
            out_specs=(pl.BlockSpec(memory_space=pltpu.VMEM),) * 3 + (pl.BlockSpec(memory_space=pltpu.HBM),),
            scratch_shapes=list(spaces.values()),
            compiler_params=pltpu.CompilerParams(
                collective_id=0, has_side_effects=True, vmem_limit_bytes=52 * 1024 * 1024),
            cost_estimate=pl.CostEstimate(
                flops=36 * heads * dim**3, bytes_accessed=5 * 1024 * 1024, transcendentals=2 * heads * dim**2),
        )(queries, keys, values, out_grad, map_weight)
        return pl.pallas_call(
            write_out,
            out_shape=shapes,
            in_specs=[pl.BlockSpec(memory_space=pltpu.VMEM)] * 3 + [pl.BlockSpec(memory_space=pltpu.HBM)],
            out_specs=(pl.BlockSpec(memory_space=pltpu.HBM),) * 4,
            scratch_shapes=[pltpu.SemaphoreType.DMA((14,)), pltpu.VMEM(map_weight.shape, F32)],
            compiler_params=pltpu.CompilerParams(vmem_limit_bytes=52 * 1024 * 1024),
        )(*grads)

    split = P("dp", "ctx", None)
    return jax.shard_map(
        per_device, mesh=mesh, in_specs=(split, split, split, split, P()),
        out_specs=(split, split, split, P()), check_vma=False)
```

```python
import functools
import math

import jax
import jax.numpy as jnp
from jax import lax
from jax.experimental import pallas as pl
from jax.experimental.pallas import tpu as pltpu
from jax.sharding import PartitionSpec as P

GROUPS = 2
F32 = jnp.float32
BF16 = jnp.bfloat16


def nn(a, b):
    return lax.dot_general(a, b, (((1,), (0,)), ((), ())), preferred_element_type=F32)


def nt(a, b):
    return lax.dot_general(a, b, (((1,), (1,)), ((), ())), preferred_element_type=F32)


def tn(a, b):
    return lax.dot_general(a, b, (((0,), (0,)), ((), ())), preferred_element_type=F32)


class Sizes:
    def __init__(self, nz, nctx, heads, dim):
        self.nz = nz
        self.chips = nctx // 2
        self.ny = math.isqrt(self.chips)
        self.heads = heads
        self.half = heads // 2
        self.groups = GROUPS
        self.hc = self.half // GROUPS
        self.dim = dim
        self.rows = dim // self.chips
        near = lambda a, size: min(a, size - a)
        self.plane = sorted(
            ((a, b) for a in range(self.ny) for b in range(self.ny) if a or b),
            key=lambda t: -near(t[0], self.ny) - near(t[1], self.ny))
        self.along = sorted(range(1, nz), key=lambda a: -near(a, nz))


def scratch(s):
    d, hc, g, n, hf = s.dim, s.hc, s.groups, s.chips, s.half
    dma = pltpu.SemaphoreType.DMA
    v = pltpu.VMEM
    wide = hf * d
    return dict(
        xin=v((4, 2, d, wide), BF16), xout=v((4, d, wide), BF16), wv=v((hf, d, d), BF16),
        swap=v((4, d, wide), F32), got=v((4, d, wide), F32),
        qf=v((2, hf, d, d), BF16), kf=v((2, hf, d, d), BF16),
        dq=v((2, hf, d, d), F32), dk=v((2, hf, d, d), F32),
        sc=v((2, hf, d, d), BF16), scaled=v((2, hf, d, d), BF16), kpre=v((2, hf, d, d), BF16),
        numer=v((2, hf, d, d), F32), denom=v((2, hf, d, 1), F32), wden=v((2, hf, d, 1), F32),
        kpart=v((2, hf, d, d), F32), vpart=v((2, hf, d, d), F32),
        own=v((3, 2, hf, d, d), F32), ksown=v((2, 2, 8, d), F32),
        comb=v((3, g, hc + 1, d, d), F32), recv=v((3, g, n, hc + 1, s.rows, d), F32),
        back=v((2, g, hc, d, d), F32), kback=v((2, 8, d), F32), mo=v((s.heads, d, d), F32),
        tsum=v((g, hc, s.rows, d), F32), zr=v((g, s.nz, s.rows, d), F32), fin=v((g, hc, s.rows, d), F32),
        outs=v((3, 2, d, wide), F32), outr=v((3, d, wide), F32),
        in_sem=dma((9,)), out_sem=dma((2, g)), sws_sem=dma((4, g)), swr_sem=dma((4, g)), met_sem=pltpu.SemaphoreType.REGULAR((2,)), os_sem=dma((3,)), or_sem=dma((3,)),
        as_sem=dma((3, g)), ar_sem=dma((3, g)),
        bs_sem=dma((3, g)), br_sem=dma((2, g)), mr_sem=dma((g, s.ny)),
        ys_sem=dma((g,)), yr_sem=dma((g,)),
        z1s_sem=dma((g,)), z1r_sem=dma((g,)), z2s_sem=dma((g,)), z2r_sem=dma((g,)),
    )


KEY, VALUE, QUERY, GRAD = range(4)


def kernel(s, names, q_hbm, k_hbm, v_hbm, g_hbm, w_hbm, qo, ko, vo, mg_hbm, *refs):
    r = dict(zip(names, refs))
    mo = r["mo"]
    n, hc, d, half, rows, ny = s.chips, s.hc, s.dim, s.half, s.rows, s.ny
    wide = half * d
    z = lax.axis_index("dp")
    ctx = lax.axis_index("ctx")
    core = lax.rem(ctx, 2)
    chip = lax.div(ctx, 2)
    cx, cy = lax.div(chip, ny), lax.rem(chip, ny)
    sibling = (z, chip * 2 + 1 - core)
    groups = range(s.groups)

    def wrap(a, size):
        return jnp.where(a >= size, a - size, a)

    def turned(a, size):
        return jnp.where(core == 0, a, (size - a) % size)

    peers = [wrap(cx + turned(a, ny), ny) * ny + wrap(cy + turned(b, ny), ny) for a, b in s.plane]
    depths = [wrap(z + turned(a, s.nz), s.nz) for a in s.along]

    def remote(src, dst, send, recv, device):
        return pltpu.make_async_remote_copy(
            src_ref=src, dst_ref=dst, send_sem=send, recv_sem=recv, device_id=device,
            device_id_type=pl.DeviceIdType.MESH)

    def wait_for(ref, sem):
        pltpu.make_async_copy(ref, ref, sem).wait()

    def rows_of(owner):
        return pl.ds(pl.multiple_of(owner * rows, rows), rows)

    def half_of(which):
        return pl.ds(pl.multiple_of(which * wide, wide), wide)

    barrier = pltpu.get_barrier_semaphore()

    def greet(device):
        pl.semaphore_signal(barrier, inc=1, device_id=device, device_id_type=pl.DeviceIdType.MESH)

    below, above = wrap(z + s.nz - 1, s.nz), wrap(z + 1, s.nz)
    near = (below, above) if s.nz > 2 else (above,)
    for to in near:
        greet((to, ctx))
    for to in peers:
        greet((z, to * 2 + core))
    greet(sibling)

    def meet(turn):
        turns = s.nz // 2 - 1
        if 1 < turn <= turns + 1:
            for i in range(2):
                pl.semaphore_wait(r["met_sem"].at[i], 1)
        if turn <= turns:
            for i, to in enumerate((above, below)):
                pl.semaphore_signal(
                    r["met_sem"].at[i], inc=1, device_id=(to, ctx), device_id_type=pl.DeviceIdType.MESH)

    inputs = (k_hbm, v_hbm, q_hbm, g_hbm)
    away = [pltpu.make_async_copy(x.at[0, :, half_of(1 - core)], r["xout"].at[a], r["in_sem"].at[a])
            for a, x in enumerate(inputs)]
    home = [pltpu.make_async_copy(x.at[0, :, half_of(core)], r["xin"].at[a, core], r["in_sem"].at[4 + a])
            for a, x in enumerate(inputs)]
    load_w = pltpu.make_async_copy(
        w_hbm.at[pl.ds(core * half, half)], r["wv"], r["in_sem"].at[8])
    for load in (away[KEY], away[VALUE], load_w, home[KEY], home[VALUE], away[QUERY], away[GRAD], home[QUERY],
                 home[GRAD]):
        load.start()
    r["ksown"][...] = jnp.zeros_like(r["ksown"])

    def swap_out(a):
        away[a].wait()
        r["swap"][a] = r["xout"][a].astype(F32)

    def swap_send(a, g):
        for part in range(2):
            at = (a, pl.ds(part * (d // 2), d // 2), pl.ds(g * hc * d, hc * d))
            remote(r["swap"].at[at], r["got"].at[at], r["sws_sem"].at[a, g], r["swr_sem"].at[a, g], sibling).start()

    def swap_in(a, g):
        at = slice(g * hc * d, (g + 1) * hc * d)
        wait_for(r["got"].at[a, :, at], r["swr_sem"].at[a, g])
        r["xin"][a, 1 - core, :, at] = r["got"][a, :, at].astype(BF16)

    place_t = lax.broadcasted_iota(jnp.int32, (d, d), 0)
    place_s = lax.broadcasted_iota(jnp.int32, (d, d), 1)
    causal = place_t >= place_s

    def block(a, b, u):
        return r["xin"][a, b, :, u * d:(u + 1) * d]

    def heads_of(g, stage, blocks=(0, 1)):
        todo = [stage(b, i, g * hc + i) for b in blocks for i in range(hc)]
        while todo:
            todo = [t for t in todo if next(t, None) is not None]

    def key_features(g, b):
        def stage(b, i, u):
            k_pre = nn(block(KEY, b, u), r["wv"][u])
            yield 1
            k_feat = jnp.where(k_pre > 0, k_pre + 1.0, jnp.exp(jnp.minimum(k_pre, 0.0)))
            kf = k_feat.astype(BF16)
            r["kf"][b, u] = kf
            r["dk"][b, u] = jnp.minimum(k_feat, 1.0)
            yield 1
            r["own"][0, b, u] = tn(kf, block(VALUE, b, u))
            r["ksown"][0, b, u:u + 1, :] = jnp.sum(kf.astype(F32), axis=0, keepdims=True)

        heads_of(g, stage, (b,))

    def tiles_of(phase, g):
        return hc + 1 if phase < 2 and g == s.groups - 1 else hc

    def send_rows(phase, g):
        tiles = tiles_of(phase, g)
        for i in range(hc):
            u = g * hc + i
            r["comb"][phase, g, i] = r["own"][phase, 0, u] + r["own"][phase, 1, u]
        if tiles > hc:
            total = r["ksown"][phase, 0] + r["ksown"][phase, 1]
            r["comb"][phase, g, hc] = jnp.concatenate([total] * (d // 8), axis=0)
        for to in peers:
            remote(r["comb"].at[phase, g, pl.ds(0, tiles), rows_of(to), :],
                   r["recv"].at[phase, g, chip, pl.ds(0, tiles)],
                   r["as_sem"].at[phase, g], r["ar_sem"].at[phase, g], (z, to * 2 + core)).start()
        r["recv"][phase, g, chip, 0:tiles] = r["comb"][phase, g, 0:tiles, rows_of(chip), :]

    def wait_rows(phase, g, sem):
        wait_for(r["recv"].at[phase, g, pl.ds(0, n - 1), pl.ds(0, tiles_of(phase, g))], sem)

    def scan(phase, g):
        wait_rows(phase, g, r["ar_sem"].at[phase, g])
        recv = r["recv"]
        acc = jnp.zeros((hc, rows, d), F32)
        for i in range(n) if phase == 0 else reversed(range(n)):
            now = recv[phase, g, i, 0:hc]
            recv[phase, g, i, 0:hc] = acc
            acc = acc + now
        for to in peers:
            remote(recv.at[phase, g, to, pl.ds(0, hc)],
                   r["back"].at[phase, g, :, rows_of(chip), :],
                   r["bs_sem"].at[phase, g], r["br_sem"].at[phase, g], (z, to * 2 + core)).start()
        r["back"][phase, g, :, rows_of(chip), :] = recv[phase, g, chip, 0:hc]
        if tiles_of(phase, g) > hc:
            ks = jnp.zeros((8, d), F32)
            for i in range(n):
                before = (chip > i) if phase == 0 else (chip < i)
                ks = ks + jnp.where(before, recv[phase, g, i, hc, 0:8, :], 0.0)
            r["kback"][phase] = ks

    def returned(phase, g):
        wait_for(r["back"].at[phase, g, :, pl.ds(0, (n - 1) * rows), :], r["br_sem"].at[phase, g])

    def state_of(phase, b, g, i):
        state = r["back"][phase, g, i]
        if b != phase:
            state = state + r["own"][phase, phase, g * hc + i]
        return state.astype(BF16)

    def sum_of(phase, b, g, i):
        u = g * hc + i
        total = r["kback"][phase, u:u + 1, :]
        if b != phase:
            total = total + r["ksown"][phase, phase, u:u + 1, :]
        return total

    def local_scores(g, blocks=(0, 1)):
        def stage(b, i, u):
            q_pre = nn(block(QUERY, b, u), r["wv"][u])
            yield 1
            q_feat = jnp.where(q_pre > 0, q_pre + 1.0, jnp.exp(jnp.minimum(q_pre, 0.0)))
            qf = q_feat.astype(BF16)
            r["qf"][b, u] = qf
            r["dq"][b, u] = jnp.minimum(q_feat, 1.0)
            yield 1
            scores = nt(qf, r["kf"][b, u])
            yield 1
            scores = jnp.where(causal, scores, 0.0)
            r["denom"][b, u] = jnp.sum(scores, axis=1, keepdims=True)
            low = scores.astype(BF16)
            r["sc"][b, u] = low
            yield 1
            r["numer"][b, u] = nn(low, block(VALUE, b, u))

        heads_of(g, stage, blocks)

    def attend(g):
        def stage(b, i, u):
            qf = r["qf"][b, u]
            grad = block(GRAD, b, u).astype(F32)
            numer = r["numer"][b, u] + nn(qf, state_of(0, b, g, i))
            qff = qf.astype(F32)
            denom = r["denom"][b, u] + jnp.sum(qff * sum_of(0, b, g, i), axis=1, keepdims=True)
            yield 1
            inv = 1.0 / denom
            scaled = (grad * inv).astype(BF16)
            r["scaled"][b, u] = scaled
            wden = -jnp.sum(grad * (numer * inv), axis=1, keepdims=True) * inv
            r["wden"][b, u] = wden
            yield 1
            r["own"][1, b, u] = tn(qf, scaled)
            r["ksown"][1, b, u:u + 1, :] = jnp.sum(wden * qff, axis=0, keepdims=True)

        heads_of(g, stage)

    def query_side(g, blocks=(0, 1)):
        def stage(b, i, u):
            wden = r["wden"][b, u]
            scaled = r["scaled"][b, u]
            mixed = nt(scaled, block(VALUE, b, u))
            yield 1
            mixed = jnp.where(causal, mixed + wden, 0.0).astype(BF16)
            yield 1
            grad = nn(mixed, r["kf"][b, u]) + nt(scaled, state_of(0, b, g, i)) + wden * sum_of(0, b, g, i)
            yield 1
            pre = (grad * r["dq"][b, u]).astype(BF16)
            yield 1
            r["outs"][0, b, :, u * d:(u + 1) * d] = nt(pre, r["wv"][u])
            r["own"][2, b, u] = tn(block(QUERY, b, u), pre)
            yield 1
            r["kpart"][b, u] = tn(mixed, r["qf"][b, u])
            r["vpart"][b, u] = tn(r["sc"][b, u], scaled)

        heads_of(g, stage, blocks)

    def key_side(g):
        def stage(b, i, u):
            grad = r["kpart"][b, u] + nt(block(VALUE, b, u), state_of(1, b, g, i)) + sum_of(1, b, g, i)
            yield 1
            pre = (grad * r["dk"][b, u]).astype(BF16)
            r["kpre"][b, u] = pre
            yield 1
            r["own"][2, b, u] = r["own"][2, b, u] + tn(block(KEY, b, u), pre)

        heads_of(g, stage)

    def key_outputs(g):
        def stage(b, i, u):
            r["outs"][1, b, :, u * d:(u + 1) * d] = nt(r["kpre"][b, u], r["wv"][u])
            r["outs"][2, b, :, u * d:(u + 1) * d] = r["vpart"][b, u] + nn(r["kf"][b, u], state_of(1, b, g, i))
            yield 1

        heads_of(g, stage)

    def give_out(a):
        remote(r["outs"].at[a, 1 - core], r["outr"].at[a], r["os_sem"].at[a], r["or_sem"].at[a], sibling).start()
        (qo, ko, vo)[a][0, :, half_of(core)] = r["outs"][a, core].astype(BF16)

    def take_out(a):
        wait_for(r["outr"].at[a], r["or_sem"].at[a])
        (qo, ko, vo)[a][0, :, half_of(1 - core)] = r["outr"][a].astype(BF16)

    def sum_chips(g):
        wait_rows(2, g, r["ar_sem"].at[2, g])
        acc = r["recv"][2, g, 0, 0:hc]
        for i in range(1, n):
            acc = acc + r["recv"][2, g, i, 0:hc]
        r["tsum"][g] = acc
        for to in depths:
            remote(r["tsum"].at[g, lax.rem(to, hc)], r["zr"].at[g, z], r["z1s_sem"].at[g],
                   r["z1r_sem"].at[g], (to, ctx)).start()
        r["zr"][g, z] = r["tsum"][g, lax.rem(z, hc)]

    def sum_docs(g):
        wait_for(r["zr"].at[g, pl.ds(0, s.nz - 1)], r["z1r_sem"].at[g])
        acc = r["zr"][g, 0]
        for i in range(1, s.nz):
            acc = acc + r["zr"][g, i]
        tile = lax.rem(z, hc)
        r["fin"][g, tile] = acc
        for off in range(-(hc // 2), hc - hc // 2):
            if off != 0:
                to = wrap(z + off % s.nz, s.nz)
                remote(r["fin"].at[g, tile], r["fin"].at[g, tile], r["z2s_sem"].at[g],
                       r["z2r_sem"].at[g], (to, ctx)).start()

    def spread(g):
        heads = pl.ds(core * half + g * hc, hc)
        if hc > 1:
            wait_for(r["fin"].at[g, pl.ds(0, hc - 1)], r["z2r_sem"].at[g])
        for to in peers:
            remote(r["fin"].at[g], mo.at[heads, rows_of(chip), :], r["bs_sem"].at[2, g],
                   r["mr_sem"].at[g, cx], (z, to * 2 + core)).start()
        mo[heads, rows_of(chip), :] = r["fin"][g]

    def strips():
        order = [0] + sorted(range(1, ny), key=lambda a: min(a, ny - a))
        for a in order:
            px = wrap(cx + a, ny)
            start = pl.multiple_of(px * (ny * rows), ny * rows)
            yield px, start, (ny if a else ny - 1)

    def collect(g):
        heads = pl.ds(core * half + g * hc, hc)
        for px, start, count in strips():
            wait_for(mo.at[heads, pl.ds(start, count * rows), :], r["mr_sem"].at[g, px])
            part = mo.at[heads, pl.ds(start, ny * rows), :]
            remote(part, part, r["ys_sem"].at[g], r["yr_sem"].at[g], sibling).start()

    def store(which, g):
        heads = pl.ds(which * half + g * hc, hc)
        return pltpu.make_async_copy(mo.at[heads], mg_hbm.at[heads], r["out_sem"].at[0 if which is core else 1, g])

    first, last = groups[:-1], s.groups - 1
    swap_out(KEY)
    swap_out(VALUE)
    load_w.wait()
    home[KEY].wait()
    home[VALUE].wait()
    for g in groups:
        key_features(g, core)
    pl.semaphore_wait(barrier, n + len(near))
    for g in groups:
        swap_send(KEY, g)
        swap_send(VALUE, g)
    turn = 0
    for g in groups:
        swap_in(KEY, g)
        swap_in(VALUE, g)
        key_features(g, 1 - core)
        send_rows(0, g)
        turn += 1
        meet(turn)
    for a in (QUERY, GRAD):
        swap_out(a)
        for g in groups:
            swap_send(a, g)
        home[a].wait()
    for g in groups:
        swap_in(QUERY, g)
    for g in first:
        local_scores(g)
        scan(0, g)
        turn += 1
        meet(turn)
    local_scores(last, (0,))
    scan(0, last)
    turn += 1
    meet(turn)
    local_scores(last, (1,))
    for g in groups:
        swap_in(GRAD, g)
    for g in groups:
        returned(0, g)
        attend(g)
        send_rows(1, g)
        turn += 1
        meet(turn)
    query_side(0)
    for g in first:
        query_side(g + 1, (0,))
        scan(1, g)
        turn += 1
        meet(turn)
        query_side(g + 1, (1,))
    scan(1, last)
    give_out(0)
    while turn < s.nz // 2:
        turn += 1
        meet(turn)
    for g in groups:
        returned(1, g)
        key_side(g)
        send_rows(2, g)
    for g in groups:
        key_outputs(g)
    give_out(1)
    give_out(2)
    for g in groups:
        sum_chips(g)
    for a in range(3):
        take_out(a)
    for a in range(4):
        for g in groups:
            wait_for(r["got"].at[a, :, pl.ds(g * hc * d, hc * d)], r["sws_sem"].at[a, g])
    for a in range(3):
        wait_for(r["outr"].at[a], r["os_sem"].at[a])
    for g in groups:
        for phase in range(3):
            wait_rows(phase, g, r["as_sem"].at[phase, g])
        for phase in range(2):
            wait_for(r["recv"].at[phase, g, pl.ds(0, n - 1), pl.ds(0, hc)], r["bs_sem"].at[phase, g])
    for g in groups:
        sum_docs(g)
    for g in groups:
        spread(g)
    for g in groups:
        collect(g)
        store(core, g).start()
    other = 1 - core
    for g in groups:
        wait_for(mo.at[pl.ds(other * half + g * hc, hc)], r["yr_sem"].at[g])
        store(other, g).start()
    for g in groups:
        wait_for(r["recv"].at[2, g, pl.ds(0, n - 1), pl.ds(0, hc)], r["bs_sem"].at[2, g])
        wait_for(mo.at[pl.ds(0, hc)], r["ys_sem"].at[g])
        wait_for(r["zr"].at[g, pl.ds(0, s.nz - 1)], r["z1s_sem"].at[g])
        if hc > 1:
            wait_for(r["fin"].at[g, pl.ds(0, hc - 1)], r["z2s_sem"].at[g])
    for g in groups:
        store(core, g).wait()
        store(other, g).wait()


def write_out(q, k, v, m, qg, kg, vg, mg, sems, held):
    size = m.shape[0] // 4
    parts = [pl.ds(part * size, size) for part in range(4)]
    reads = [pltpu.make_async_copy(m.at[at], held.at[at], sems.at[i]) for i, at in enumerate(parts)]
    writes = [pltpu.make_async_copy(held.at[at], mg.at[at], sems.at[4 + i]) for i, at in enumerate(parts)]
    rows = q.shape[1] // 2
    for src, dst in ((q, qg), (k, kg), (v, vg)):
        for part in range(2):
            at = pl.ds(part * rows, rows)
            writes.append(pltpu.make_async_copy(src.at[0, at], dst.at[0, at], sems.at[4 + len(writes)]))
    for copy in reads + writes[4:]:
        copy.start()
    for read, write in zip(reads, writes):
        read.wait()
        write.start()
    for copy in writes:
        copy.wait()


def solution(mesh):
    nz, nctx = mesh.shape["dp"], mesh.shape["ctx"]

    def per_device(queries, keys, values, out_grad, map_weight):
        heads, dim = map_weight.shape[0], map_weight.shape[1]
        s = Sizes(nz, nctx, heads, dim)
        spaces = scratch(s)
        act = jax.ShapeDtypeStruct(queries.shape, BF16)
        shapes = (act, act, act, jax.ShapeDtypeStruct(map_weight.shape, F32))
        grads = pl.pallas_call(
            functools.partial(kernel, s, tuple(spaces)),
            out_shape=shapes,
            in_specs=[pl.BlockSpec(memory_space=pltpu.HBM)] * 5,
            out_specs=(pl.BlockSpec(memory_space=pltpu.VMEM),) * 3 + (pl.BlockSpec(memory_space=pltpu.HBM),),
            scratch_shapes=list(spaces.values()),
            compiler_params=pltpu.CompilerParams(
                collective_id=0, has_side_effects=True, vmem_limit_bytes=52 * 1024 * 1024),
            cost_estimate=pl.CostEstimate(
                flops=36 * heads * dim**3, bytes_accessed=5 * 1024 * 1024, transcendentals=2 * heads * dim**2),
        )(queries, keys, values, out_grad, map_weight)
        return pl.pallas_call(
            write_out,
            out_shape=shapes,
            in_specs=[pl.BlockSpec(memory_space=pltpu.VMEM)] * 3 + [pl.BlockSpec(memory_space=pltpu.HBM)],
            out_specs=(pl.BlockSpec(memory_space=pltpu.HBM),) * 4,
            scratch_shapes=[pltpu.SemaphoreType.DMA((14,)), pltpu.VMEM(map_weight.shape, F32)],
            compiler_params=pltpu.CompilerParams(vmem_limit_bytes=52 * 1024 * 1024),
        )(*grads)

    split = P("dp", "ctx", None)
    return jax.shard_map(
        per_device, mesh=mesh, in_specs=(split, split, split, split, P()),
        out_specs=(split, split, split, P()), check_vma=False)
```

```python
import functools
import math

import jax
import jax.numpy as jnp
from jax import lax
from jax.experimental import pallas as pl
from jax.experimental.pallas import tpu as pltpu
from jax.sharding import PartitionSpec as P

GROUPS = 2
F32 = jnp.float32
BF16 = jnp.bfloat16


def nn(a, b):
    return lax.dot_general(a, b, (((1,), (0,)), ((), ())), preferred_element_type=F32)


def nt(a, b):
    return lax.dot_general(a, b, (((1,), (1,)), ((), ())), preferred_element_type=F32)


def tn(a, b):
    return lax.dot_general(a, b, (((0,), (0,)), ((), ())), preferred_element_type=F32)


class Sizes:
    def __init__(self, nz, nctx, heads, dim):
        self.nz = nz
        self.chips = nctx // 2
        self.ny = math.isqrt(self.chips)
        self.heads = heads
        self.half = heads // 2
        self.groups = GROUPS
        self.hc = self.half // GROUPS
        self.dim = dim
        self.rows = dim // self.chips
        near = lambda a, size: min(a, size - a)
        self.plane = sorted(
            ((a, b) for a in range(self.ny) for b in range(self.ny) if a or b),
            key=lambda t: -near(t[0], self.ny) - near(t[1], self.ny))
        self.along = sorted(range(1, nz), key=lambda a: -near(a, nz))


def scratch(s):
    d, hc, g, n, hf = s.dim, s.hc, s.groups, s.chips, s.half
    dma = pltpu.SemaphoreType.DMA
    v = pltpu.VMEM
    wide = hf * d
    return dict(
        xin=v((4, 2, d, wide), BF16), xout=v((4, d, wide), BF16), wv=v((hf, d, d), BF16),
        swap=v((4, d, wide), F32), got=v((4, d, wide), F32),
        qf=v((2, hf, d, d), BF16), kf=v((2, hf, d, d), BF16),
        dq=v((2, hf, d, d), F32), dk=v((2, hf, d, d), F32),
        sc=v((2, hf, d, d), BF16), scaled=v((2, hf, d, d), BF16), kpre=v((2, hf, d, d), BF16),
        numer=v((2, hf, d, d), F32), denom=v((2, hf, d, 1), F32), wden=v((2, hf, d, 1), F32),
        kpart=v((2, hf, d, d), F32), vpart=v((2, hf, d, d), F32),
        own=v((3, 2, hf, d, d), F32), ksown=v((2, 2, 8, d), F32),
        comb=v((3, g, hc + 1, d, d), F32), recv=v((3, g, n, hc + 1, s.rows, d), F32),
        back=v((2, g, hc, d, d), F32), kback=v((2, 8, d), F32), mo=v((s.heads, d, d), F32),
        tsum=v((g, hc, s.rows, d), F32), zr=v((g, s.nz, s.rows, d), F32), fin=v((g, hc, s.rows, d), F32),
        outs=v((3, 2, d, wide), F32), outr=v((3, d, wide), F32),
        in_sem=dma((9,)), out_sem=dma((2, g)), sws_sem=dma((4, g)), swr_sem=dma((4, g)), met_sem=pltpu.SemaphoreType.REGULAR((2,)), os_sem=dma((3,)), or_sem=dma((3,)),
        as_sem=dma((3, g)), ar_sem=dma((3, g)),
        bs_sem=dma((3, g)), br_sem=dma((2, g)), mr_sem=dma((g, s.ny)),
        ys_sem=dma((g,)), yr_sem=dma((g,)),
        z1s_sem=dma((g,)), z1r_sem=dma((g,)), z2s_sem=dma((g,)), z2r_sem=dma((g,)),
    )


KEY, VALUE, QUERY, GRAD = range(4)


def kernel(s, names, q_hbm, k_hbm, v_hbm, g_hbm, w_hbm, qo, ko, vo, mg_hbm, *refs):
    r = dict(zip(names, refs))
    mo = r["mo"]
    n, hc, d, half, rows, ny = s.chips, s.hc, s.dim, s.half, s.rows, s.ny
    wide = half * d
    z = lax.axis_index("dp")
    ctx = lax.axis_index("ctx")
    core = lax.rem(ctx, 2)
    chip = lax.div(ctx, 2)
    cx, cy = lax.div(chip, ny), lax.rem(chip, ny)
    sibling = (z, chip * 2 + 1 - core)
    groups = range(s.groups)

    def wrap(a, size):
        return jnp.where(a >= size, a - size, a)

    def turned(a, size):
        return jnp.where(core == 0, a, (size - a) % size)

    peers = [wrap(cx + turned(a, ny), ny) * ny + wrap(cy + turned(b, ny), ny) for a, b in s.plane]
    depths = [wrap(z + turned(a, s.nz), s.nz) for a in s.along]

    def remote(src, dst, send, recv, device):
        return pltpu.make_async_remote_copy(
            src_ref=src, dst_ref=dst, send_sem=send, recv_sem=recv, device_id=device,
            device_id_type=pl.DeviceIdType.MESH)

    def wait_for(ref, sem):
        pltpu.make_async_copy(ref, ref, sem).wait()

    def rows_of(owner):
        return pl.ds(pl.multiple_of(owner * rows, rows), rows)

    def half_of(which):
        return pl.ds(pl.multiple_of(which * wide, wide), wide)

    barrier = pltpu.get_barrier_semaphore()

    def greet(device):
        pl.semaphore_signal(barrier, inc=1, device_id=device, device_id_type=pl.DeviceIdType.MESH)

    below, above = wrap(z + s.nz - 1, s.nz), wrap(z + 1, s.nz)
    near = (below, above) if s.nz > 2 else (above,)
    for to in near:
        greet((to, ctx))
    for to in peers:
        greet((z, to * 2 + core))
    greet(sibling)

    def meet(turn):
        turns = s.nz // 2 - 1
        if 1 < turn <= turns + 1:
            for i in range(2):
                pl.semaphore_wait(r["met_sem"].at[i], 1)
        if turn <= turns:
            for i, to in enumerate((above, below)):
                pl.semaphore_signal(
                    r["met_sem"].at[i], inc=1, device_id=(to, ctx), device_id_type=pl.DeviceIdType.MESH)

    inputs = (k_hbm, v_hbm, q_hbm, g_hbm)
    away = [pltpu.make_async_copy(x.at[0, :, half_of(1 - core)], r["xout"].at[a], r["in_sem"].at[a])
            for a, x in enumerate(inputs)]
    home = [pltpu.make_async_copy(x.at[0, :, half_of(core)], r["xin"].at[a, core], r["in_sem"].at[4 + a])
            for a, x in enumerate(inputs)]
    load_w = pltpu.make_async_copy(
        w_hbm.at[pl.ds(core * half, half)], r["wv"], r["in_sem"].at[8])
    for load in (away[KEY], away[VALUE], load_w, home[KEY], home[VALUE], away[QUERY], away[GRAD], home[QUERY],
                 home[GRAD]):
        load.start()
    r["ksown"][...] = jnp.zeros_like(r["ksown"])

    def swap_out(a):
        away[a].wait()
        r["swap"][a] = r["xout"][a].astype(F32)

    def swap_send(a, g):
        for part in range(2):
            at = (a, pl.ds(part * (d // 2), d // 2), pl.ds(g * hc * d, hc * d))
            remote(r["swap"].at[at], r["got"].at[at], r["sws_sem"].at[a, g], r["swr_sem"].at[a, g], sibling).start()

    def swap_in(a, g):
        at = slice(g * hc * d, (g + 1) * hc * d)
        wait_for(r["got"].at[a, :, at], r["swr_sem"].at[a, g])
        r["xin"][a, 1 - core, :, at] = r["got"][a, :, at].astype(BF16)

    place_t = lax.broadcasted_iota(jnp.int32, (d, d), 0)
    place_s = lax.broadcasted_iota(jnp.int32, (d, d), 1)
    causal = place_t >= place_s

    def block(a, b, u):
        return r["xin"][a, b, :, u * d:(u + 1) * d]

    def heads_of(g, stage, blocks=(0, 1)):
        todo = [stage(b, i, g * hc + i) for b in blocks for i in range(hc)]
        while todo:
            todo = [t for t in todo if next(t, None) is not None]

    def key_features(g, b):
        def stage(b, i, u):
            k_pre = nn(block(KEY, b, u), r["wv"][u])
            yield 1
            k_feat = jnp.where(k_pre > 0, k_pre + 1.0, jnp.exp(jnp.minimum(k_pre, 0.0)))
            kf = k_feat.astype(BF16)
            r["kf"][b, u] = kf
            r["dk"][b, u] = jnp.minimum(k_feat, 1.0)
            yield 1
            r["own"][0, b, u] = tn(kf, block(VALUE, b, u))
            r["ksown"][0, b, u:u + 1, :] = jnp.sum(kf.astype(F32), axis=0, keepdims=True)

        heads_of(g, stage, (b,))

    def tiles_of(phase, g):
        return hc + 1 if phase < 2 and g == s.groups - 1 else hc

    def send_rows(phase, g):
        tiles = tiles_of(phase, g)
        for i in range(hc):
            u = g * hc + i
            r["comb"][phase, g, i] = r["own"][phase, 0, u] + r["own"][phase, 1, u]
        if tiles > hc:
            total = r["ksown"][phase, 0] + r["ksown"][phase, 1]
            r["comb"][phase, g, hc] = jnp.concatenate([total] * (d // 8), axis=0)
        for to in peers:
            remote(r["comb"].at[phase, g, pl.ds(0, tiles), rows_of(to), :],
                   r["recv"].at[phase, g, chip, pl.ds(0, tiles)],
                   r["as_sem"].at[phase, g], r["ar_sem"].at[phase, g], (z, to * 2 + core)).start()
        r["recv"][phase, g, chip, 0:tiles] = r["comb"][phase, g, 0:tiles, rows_of(chip), :]

    def wait_rows(phase, g, sem):
        wait_for(r["recv"].at[phase, g, pl.ds(0, n - 1), pl.ds(0, tiles_of(phase, g))], sem)

    def scan(phase, g):
        wait_rows(phase, g, r["ar_sem"].at[phase, g])
        recv = r["recv"]
        acc = jnp.zeros((hc, rows, d), F32)
        for i in range(n) if phase == 0 else reversed(range(n)):
            now = recv[phase, g, i, 0:hc]
            recv[phase, g, i, 0:hc] = acc
            acc = acc + now
        for to in peers:
            remote(recv.at[phase, g, to, pl.ds(0, hc)],
                   r["back"].at[phase, g, :, rows_of(chip), :],
                   r["bs_sem"].at[phase, g], r["br_sem"].at[phase, g], (z, to * 2 + core)).start()
        r["back"][phase, g, :, rows_of(chip), :] = recv[phase, g, chip, 0:hc]
        if tiles_of(phase, g) > hc:
            ks = jnp.zeros((8, d), F32)
            for i in range(n):
                before = (chip > i) if phase == 0 else (chip < i)
                ks = ks + jnp.where(before, recv[phase, g, i, hc, 0:8, :], 0.0)
            r["kback"][phase] = ks

    def returned(phase, g):
        wait_for(r["back"].at[phase, g, :, pl.ds(0, (n - 1) * rows), :], r["br_sem"].at[phase, g])

    def state_of(phase, b, g, i):
        state = r["back"][phase, g, i]
        if b != phase:
            state = state + r["own"][phase, phase, g * hc + i]
        return state.astype(BF16)

    def sum_of(phase, b, g, i):
        u = g * hc + i
        total = r["kback"][phase, u:u + 1, :]
        if b != phase:
            total = total + r["ksown"][phase, phase, u:u + 1, :]
        return total

    def local_scores(g, blocks=(0, 1)):
        def stage(b, i, u):
            q_pre = nn(block(QUERY, b, u), r["wv"][u])
            yield 1
            q_feat = jnp.where(q_pre > 0, q_pre + 1.0, jnp.exp(jnp.minimum(q_pre, 0.0)))
            qf = q_feat.astype(BF16)
            r["qf"][b, u] = qf
            r["dq"][b, u] = jnp.minimum(q_feat, 1.0)
            yield 1
            scores = nt(qf, r["kf"][b, u])
            yield 1
            scores = jnp.where(causal, scores, 0.0)
            r["denom"][b, u] = jnp.sum(scores, axis=1, keepdims=True)
            low = scores.astype(BF16)
            r["sc"][b, u] = low
            yield 1
            r["numer"][b, u] = nn(low, block(VALUE, b, u))

        heads_of(g, stage, blocks)

    def attend(g):
        def stage(b, i, u):
            qf = r["qf"][b, u]
            grad = block(GRAD, b, u).astype(F32)
            numer = r["numer"][b, u] + nn(qf, state_of(0, b, g, i))
            qff = qf.astype(F32)
            denom = r["denom"][b, u] + jnp.sum(qff * sum_of(0, b, g, i), axis=1, keepdims=True)
            yield 1
            inv = 1.0 / denom
            scaled = (grad * inv).astype(BF16)
            r["scaled"][b, u] = scaled
            wden = -jnp.sum(grad * (numer * inv), axis=1, keepdims=True) * inv
            r["wden"][b, u] = wden
            yield 1
            r["own"][1, b, u] = tn(qf, scaled)
            r["ksown"][1, b, u:u + 1, :] = jnp.sum(wden * qff, axis=0, keepdims=True)

        heads_of(g, stage)

    def query_side(g, blocks=(0, 1)):
        def stage(b, i, u):
            wden = r["wden"][b, u]
            scaled = r["scaled"][b, u]
            mixed = nt(scaled, block(VALUE, b, u))
            yield 1
            mixed = jnp.where(causal, mixed + wden, 0.0).astype(BF16)
            yield 1
            grad = nn(mixed, r["kf"][b, u]) + nt(scaled, state_of(0, b, g, i)) + wden * sum_of(0, b, g, i)
            yield 1
            pre = (grad * r["dq"][b, u]).astype(BF16)
            yield 1
            r["outs"][0, b, :, u * d:(u + 1) * d] = nt(pre, r["wv"][u])
            r["own"][2, b, u] = tn(block(QUERY, b, u), pre)
            yield 1
            r["kpart"][b, u] = tn(mixed, r["qf"][b, u])
            r["vpart"][b, u] = tn(r["sc"][b, u], scaled)

        heads_of(g, stage, blocks)

    def key_side(g):
        def stage(b, i, u):
            grad = r["kpart"][b, u] + nt(block(VALUE, b, u), state_of(1, b, g, i)) + sum_of(1, b, g, i)
            yield 1
            pre = (grad * r["dk"][b, u]).astype(BF16)
            r["kpre"][b, u] = pre
            yield 1
            r["own"][2, b, u] = r["own"][2, b, u] + tn(block(KEY, b, u), pre)

        heads_of(g, stage)

    def key_outputs(g):
        def stage(b, i, u):
            r["outs"][1, b, :, u * d:(u + 1) * d] = nt(r["kpre"][b, u], r["wv"][u])
            r["outs"][2, b, :, u * d:(u + 1) * d] = r["vpart"][b, u] + nn(r["kf"][b, u], state_of(1, b, g, i))
            yield 1

        heads_of(g, stage)

    def give_out(a):
        remote(r["outs"].at[a, 1 - core], r["outr"].at[a], r["os_sem"].at[a], r["or_sem"].at[a], sibling).start()
        (qo, ko, vo)[a][0, :, half_of(core)] = r["outs"][a, core].astype(BF16)

    def take_out(a):
        wait_for(r["outr"].at[a], r["or_sem"].at[a])
        (qo, ko, vo)[a][0, :, half_of(1 - core)] = r["outr"][a].astype(BF16)

    def sum_chips(g):
        wait_rows(2, g, r["ar_sem"].at[2, g])
        acc = r["recv"][2, g, 0, 0:hc]
        for i in range(1, n):
            acc = acc + r["recv"][2, g, i, 0:hc]
        r["tsum"][g] = acc
        for to in depths:
            remote(r["tsum"].at[g, lax.rem(to, hc)], r["zr"].at[g, z], r["z1s_sem"].at[g],
                   r["z1r_sem"].at[g], (to, ctx)).start()
        r["zr"][g, z] = r["tsum"][g, lax.rem(z, hc)]

    def sum_docs(g):
        wait_for(r["zr"].at[g, pl.ds(0, s.nz - 1)], r["z1r_sem"].at[g])
        acc = r["zr"][g, 0]
        for i in range(1, s.nz):
            acc = acc + r["zr"][g, i]
        tile = lax.rem(z, hc)
        r["fin"][g, tile] = acc
        for off in range(-(hc // 2), hc - hc // 2):
            if off != 0:
                to = wrap(z + turned(off % s.nz, s.nz), s.nz)
                remote(r["fin"].at[g, tile], r["fin"].at[g, tile], r["z2s_sem"].at[g],
                       r["z2r_sem"].at[g], (to, ctx)).start()

    def spread(g):
        heads = pl.ds(core * half + g * hc, hc)
        if hc > 1:
            wait_for(r["fin"].at[g, pl.ds(0, hc - 1)], r["z2r_sem"].at[g])
        for to in peers:
            remote(r["fin"].at[g], mo.at[heads, rows_of(chip), :], r["bs_sem"].at[2, g],
                   r["mr_sem"].at[g, cx], (z, to * 2 + core)).start()
        mo[heads, rows_of(chip), :] = r["fin"][g]

    def strips():
        order = [0] + sorted(range(1, ny), key=lambda a: min(a, ny - a))
        for a in order:
            px = wrap(cx + a, ny)
            start = pl.multiple_of(px * (ny * rows), ny * rows)
            yield px, start, (ny if a else ny - 1)

    def collect(g):
        heads = pl.ds(core * half + g * hc, hc)
        for px, start, count in strips():
            wait_for(mo.at[heads, pl.ds(start, count * rows), :], r["mr_sem"].at[g, px])
            part = mo.at[heads, pl.ds(start, ny * rows), :]
            remote(part, part, r["ys_sem"].at[g], r["yr_sem"].at[g], sibling).start()

    def store(which, g):
        heads = pl.ds(which * half + g * hc, hc)
        return pltpu.make_async_copy(mo.at[heads], mg_hbm.at[heads], r["out_sem"].at[0 if which is core else 1, g])

    first, last = groups[:-1], s.groups - 1
    swap_out(KEY)
    swap_out(VALUE)
    load_w.wait()
    home[KEY].wait()
    home[VALUE].wait()
    for g in groups:
        key_features(g, core)
    pl.semaphore_wait(barrier, n + len(near))
    for g in groups:
        swap_send(KEY, g)
        swap_send(VALUE, g)
    turn = 0
    for g in groups:
        swap_in(KEY, g)
        swap_in(VALUE, g)
        key_features(g, 1 - core)
        send_rows(0, g)
        turn += 1
        meet(turn)
    for a in (QUERY, GRAD):
        swap_out(a)
        for g in groups:
            swap_send(a, g)
        home[a].wait()
    for g in groups:
        swap_in(QUERY, g)
    for g in first:
        local_scores(g)
        scan(0, g)
        turn += 1
        meet(turn)
    local_scores(last, (0,))
    scan(0, last)
    turn += 1
    meet(turn)
    local_scores(last, (1,))
    for g in groups:
        swap_in(GRAD, g)
    for g in groups:
        returned(0, g)
        attend(g)
        send_rows(1, g)
        turn += 1
        meet(turn)
    query_side(0)
    for g in first:
        query_side(g + 1, (0,))
        scan(1, g)
        turn += 1
        meet(turn)
        query_side(g + 1, (1,))
    scan(1, last)
    give_out(0)
    while turn < s.nz // 2:
        turn += 1
        meet(turn)
    for g in groups:
        returned(1, g)
        key_side(g)
        send_rows(2, g)
    for g in groups:
        key_outputs(g)
    give_out(1)
    give_out(2)
    for g in groups:
        sum_chips(g)
    for a in range(3):
        take_out(a)
    for a in range(4):
        for g in groups:
            wait_for(r["got"].at[a, :, pl.ds(g * hc * d, hc * d)], r["sws_sem"].at[a, g])
    for a in range(3):
        wait_for(r["outr"].at[a], r["os_sem"].at[a])
    for g in groups:
        for phase in range(3):
            wait_rows(phase, g, r["as_sem"].at[phase, g])
        for phase in range(2):
            wait_for(r["recv"].at[phase, g, pl.ds(0, n - 1), pl.ds(0, hc)], r["bs_sem"].at[phase, g])
    for g in groups:
        sum_docs(g)
    for g in groups:
        spread(g)
    for g in groups:
        collect(g)
        store(core, g).start()
    other = 1 - core
    for g in groups:
        wait_for(mo.at[pl.ds(other * half + g * hc, hc)], r["yr_sem"].at[g])
        store(other, g).start()
    for g in groups:
        wait_for(r["recv"].at[2, g, pl.ds(0, n - 1), pl.ds(0, hc)], r["bs_sem"].at[2, g])
        wait_for(mo.at[pl.ds(0, hc)], r["ys_sem"].at[g])
        wait_for(r["zr"].at[g, pl.ds(0, s.nz - 1)], r["z1s_sem"].at[g])
        if hc > 1:
            wait_for(r["fin"].at[g, pl.ds(0, hc - 1)], r["z2s_sem"].at[g])
    for g in groups:
        store(core, g).wait()
        store(other, g).wait()


def write_out(q, k, v, m, qg, kg, vg, mg, sems, held):
    size = m.shape[0] // 4
    parts = [pl.ds(part * size, size) for part in range(4)]
    reads = [pltpu.make_async_copy(m.at[at], held.at[at], sems.at[i]) for i, at in enumerate(parts)]
    writes = [pltpu.make_async_copy(held.at[at], mg.at[at], sems.at[4 + i]) for i, at in enumerate(parts)]
    rows = q.shape[1] // 2
    for src, dst in ((q, qg), (k, kg), (v, vg)):
        for part in range(2):
            at = pl.ds(part * rows, rows)
            writes.append(pltpu.make_async_copy(src.at[0, at], dst.at[0, at], sems.at[4 + len(writes)]))
    for copy in reads + writes[4:]:
        copy.start()
    for read, write in zip(reads, writes):
        read.wait()
        write.start()
    for copy in writes:
        copy.wait()


def solution(mesh):
    nz, nctx = mesh.shape["dp"], mesh.shape["ctx"]

    def per_device(queries, keys, values, out_grad, map_weight):
        heads, dim = map_weight.shape[0], map_weight.shape[1]
        s = Sizes(nz, nctx, heads, dim)
        spaces = scratch(s)
        act = jax.ShapeDtypeStruct(queries.shape, BF16)
        shapes = (act, act, act, jax.ShapeDtypeStruct(map_weight.shape, F32))
        grads = pl.pallas_call(
            functools.partial(kernel, s, tuple(spaces)),
            out_shape=shapes,
            in_specs=[pl.BlockSpec(memory_space=pltpu.HBM)] * 5,
            out_specs=(pl.BlockSpec(memory_space=pltpu.VMEM),) * 3 + (pl.BlockSpec(memory_space=pltpu.HBM),),
            scratch_shapes=list(spaces.values()),
            compiler_params=pltpu.CompilerParams(
                collective_id=0, has_side_effects=True, vmem_limit_bytes=52 * 1024 * 1024),
            cost_estimate=pl.CostEstimate(
                flops=36 * heads * dim**3, bytes_accessed=5 * 1024 * 1024, transcendentals=2 * heads * dim**2),
        )(queries, keys, values, out_grad, map_weight)
        return pl.pallas_call(
            write_out,
            out_shape=shapes,
            in_specs=[pl.BlockSpec(memory_space=pltpu.VMEM)] * 3 + [pl.BlockSpec(memory_space=pltpu.HBM)],
            out_specs=(pl.BlockSpec(memory_space=pltpu.HBM),) * 4,
            scratch_shapes=[pltpu.SemaphoreType.DMA((14,)), pltpu.VMEM(map_weight.shape, F32)],
            compiler_params=pltpu.CompilerParams(vmem_limit_bytes=52 * 1024 * 1024),
        )(*grads)

    split = P("dp", "ctx", None)
    return jax.shard_map(
        per_device, mesh=mesh, in_specs=(split, split, split, split, P()),
        out_specs=(split, split, split, P()), check_vma=False)
```
